512 devices in a mesh: dp: 32 (over y_lo, x, core), seq: 16 (over z, y_hi).
Axes of the slice: x: 4, y: 8 (y_hi: 2, y_lo: 4; y = y_hi * 4 + y_lo), z: 8, core: 2. Of those that a mesh axis runs over, the one named last changes fastest.
Arguments:
- tokens: bfloat16 [32, 2048, 1024], P('dp', 'seq'), may hold values from -8 to 8
- qkv_weight: bfloat16 [16, 192, 1024], P('seq', 'dp'), may hold values from -0.18 to 0.18
- key_tiles: int32 [32, 16, 4], P('dp'), may hold values from 0 to 15, as said below
- key_counts: int32 [32, 16], P('dp'), may hold values from 1 to 4, as said below
- cotangent: bfloat16 [32, 2048, 1024], P('dp', 'seq'), may hold values from -6 to 6
Outputs:
- attended: bfloat16 [32, 2048, 1024], P('dp', 'seq')
- grad_input: bfloat16 [32, 2048, 1024], P('dp', 'seq')
- grad_weight: float32 [16, 192, 1024], P('seq', 'dp')
The draws below stay inside these ranges and needn't reach their ends.
Inputs may be any that keep to these rules, and one draw needn't show every extreme that they name: `key_tiles`: row a of a scene lists tile a first, then 4 - 1 other tiles; the 4 entries of a row are distinct, and those beyond the count are ignored. `key_counts`: some query tile of every scene has a count of 4.
All inputs are finite; a program needn't handle non-finite values.
Results may differ from the reference program's by a relative error of at most 0.025.
Values may be sent and summed in bfloat16 or wider, within the bound.
No kernel may reach another device: no remote copies, remote signals or barrier semaphores. Data moves between devices by JAX's collectives and lax.ppermute only.
A program may use at most 64 MiB of HBM per device.

```python
import jax
import jax.numpy as jnp
from jax import lax

D = 1024
HEADS = 16
HEAD_DIM = 64
TILE = 128
TOP = 4
SCENES = 32
SEQ_LEN = 2048
TILES = 16


def draw_tokens(key, part):
    base = jax.random.normal(key, (SCENES, SEQ_LEN, D), jnp.float32)
    return jnp.clip(base, -8.0, 8.0).astype(jnp.bfloat16)


def draw_qkv_weight(key, part):
    weight = jax.random.normal(key, (HEADS, 3 * HEAD_DIM, D), jnp.float32) * D ** (-0.5)
    return jnp.clip(weight, -0.18, 0.18).astype(jnp.bfloat16)


def draw_key_tiles(key, part):
    ranks = jax.random.randint(key, (SCENES, TILES, TILES), 0, 65536) * TILES
    ranks = ranks + jnp.arange(TILES, dtype=jnp.int32)[None, None, :]
    own = jnp.arange(TILES, dtype=jnp.int32)
    ranks = jnp.where(own[None, :, None] == own[None, None, :], 1 << 30, ranks)
    others = jnp.argsort(ranks, axis=-1, stable=True)[:, :, :TOP - 1].astype(jnp.int32)
    first = jnp.broadcast_to(own[None, :, None], (SCENES, TILES, 1))
    return jnp.concatenate([first, others], axis=-1)


def draw_key_counts(key, part):
    counts = jax.random.randint(key, (SCENES, TILES), 1, TOP + 1)
    position = jnp.arange(TILES, dtype=jnp.int32)[None, :]
    return jnp.where(position == 0, TOP, counts).astype(jnp.int32)


def level_of(own_key, shape, cuts, least, high):
    level, own = 1.0, jax.random.fold_in(own_key, 6)
    for dim, parts in cuts:
        steps = jnp.exp(jax.random.uniform(jax.random.fold_in(own, dim), (parts,), jnp.float32, least / len(cuts), high / len(cuts)))
        level = level * jnp.repeat(steps, shape[dim] // parts).reshape([-1 if axis == dim else 1 for axis in range(len(shape))])
    return level


def gaussian(own_key, shape, width, bound, pieces=(), kind=jnp.bfloat16):
    array = jax.random.normal(own_key, shape, jnp.float32) * width
    if len(pieces) > 0:
        array = level_of(own_key, shape, pieces, -0.22, 0.18) * array
    return jnp.clip(array, min=-bound, max=bound).astype(kind)


def setup_inputs(seed: int = 0) -> dict:
    arg_keys = jax.random.split(jax.random.key(seed), 6)
    tokens = draw_tokens(jax.random.fold_in(arg_keys[5], 71), 0)
    qkv_weight = draw_qkv_weight(jax.random.fold_in(arg_keys[5], 71), 0)
    key_tiles = draw_key_tiles(jax.random.fold_in(arg_keys[5], 71), 0)
    key_counts = draw_key_counts(jax.random.fold_in(arg_keys[5], 71), 0)
    cotangent = gaussian(arg_keys[4], (SCENES, SEQ_LEN, D), 1.0, 6.0, ((0, 32), (1, 16)))
    return dict(tokens=tokens, qkv_weight=qkv_weight, key_tiles=key_tiles, key_counts=key_counts, cotangent=cotangent)


def scene_pass(scene_tokens, scene_grad, tile_list, tile_count, weight):
    scale = HEAD_DIM ** -0.5
    qkv = jnp.einsum('ld,hfd->lhf', scene_tokens.astype(jnp.float32), weight.astype(jnp.float32)).astype(jnp.bfloat16)
    shape_tiles = (TILES, TILE, HEADS, HEAD_DIM)
    query = qkv[:, :, :HEAD_DIM].reshape(shape_tiles).astype(jnp.float32)
    keys = qkv[:, :, HEAD_DIM:2 * HEAD_DIM].reshape(shape_tiles)
    values = qkv[:, :, 2 * HEAD_DIM:].reshape(shape_tiles)
    key_sel = keys[tile_list].astype(jnp.float32)
    value_sel = values[tile_list].astype(jnp.float32)
    live = jnp.arange(TOP, dtype=jnp.int32)[None, :] < tile_count[:, None]
    live = live[:, None, None, :, None]
    scores = jnp.einsum('aqhd,atkhd->ahqtk', query, key_sel) * scale
    scores = jnp.where(live, scores, -1e30)
    top_score = jnp.max(scores, axis=(3, 4), keepdims=True)
    expo = jnp.exp(scores - top_score)
    probs = expo / jnp.sum(expo, axis=(3, 4), keepdims=True)
    probs_b = probs.astype(jnp.bfloat16).astype(jnp.float32)
    output = jnp.einsum('ahqtk,atkhd->aqhd', probs_b, value_sel).astype(jnp.bfloat16)
    grad_t = scene_grad.reshape(shape_tiles).astype(jnp.float32)
    dprobs = jnp.einsum('aqhd,atkhd->ahqtk', grad_t, value_sel)
    delta = jnp.sum(probs * dprobs, axis=(3, 4), keepdims=True)
    dscores = (probs * (dprobs - delta) * scale).astype(jnp.bfloat16).astype(jnp.float32)
    dquery = jnp.einsum('ahqtk,atkhd->aqhd', dscores, key_sel).astype(jnp.bfloat16)
    dkey_part = jnp.einsum('ahqtk,aqhd->atkhd', dscores, query)
    dvalue_part = jnp.einsum('ahqtk,aqhd->atkhd', probs_b, grad_t)
    flat = tile_list.reshape(-1)
    part_shape = (TILES * TOP, TILE, HEADS, HEAD_DIM)
    dkey = jnp.zeros(shape_tiles, jnp.float32).at[flat].add(dkey_part.reshape(part_shape)).astype(jnp.bfloat16)
    dvalue = jnp.zeros(shape_tiles, jnp.float32).at[flat].add(dvalue_part.reshape(part_shape)).astype(jnp.bfloat16)
    dqkv = jnp.concatenate([dquery, dkey, dvalue], axis=-1).reshape(SEQ_LEN, HEADS, 3 * HEAD_DIM)
    dqkv_f = dqkv.astype(jnp.float32)
    grad_in = jnp.einsum('lhf,hfd->ld', dqkv_f, weight.astype(jnp.float32)).astype(jnp.bfloat16)
    grad_w = jnp.einsum('lhf,ld->hfd', dqkv_f, scene_tokens.astype(jnp.float32))
    return output.reshape(SEQ_LEN, D), grad_in, grad_w


def reference(tokens, qkv_weight, key_tiles, key_counts, cotangent):
    def step(total, items):
        scene_tokens, scene_grad, tile_list, tile_count = items
        output, grad_in, grad_w = scene_pass(scene_tokens, scene_grad, tile_list, tile_count, qkv_weight)
        return total + grad_w, (output, grad_in)

    start = jnp.zeros((HEADS, 3 * HEAD_DIM, D), jnp.float32)
    total, outs = lax.scan(step, start, (tokens, cotangent, key_tiles, key_counts))
    grad_weight = total * ((SCENES * SEQ_LEN) ** -0.5)
    return outs[0], outs[1], grad_weight
```

```python
import functools

import jax
import jax.numpy as jnp
from jax import lax
from jax.experimental import pallas as pl
from jax.experimental.pallas import tpu as pltpu
from jax.sharding import PartitionSpec as P

HEAD_DIM = 64
TILE = 128
TOP = 4
BF = jnp.bfloat16
F32 = jnp.float32
VM = pl.BlockSpec(memory_space=pltpu.VMEM)
SM = pl.BlockSpec(memory_space=pltpu.SMEM)
PARAMS = pltpu.CompilerParams(vmem_limit_bytes=48 * 2**20)

YL, XN, CORES, ZN, YH = 4, 4, 2, 8, 2
DP = YL * XN * CORES
SEQ = ZN * YH


def dot(a, b, ca, cb):
    return lax.dot_general(a, b, (((ca,), (cb,)), ((), ())), preferred_element_type=F32)


def flip_y(x):
    return lax.ppermute(x, "seq", [(s, s ^ 1) for s in range(SEQ)])


def shift_z(x, k):
    return lax.ppermute(x, "seq", [(s, (s + YH * k) % SEQ) for s in range(SEQ)])


def swap_core(x):
    return lax.ppermute(x, "dp", [(d, d ^ 1) for d in range(DP)])


def shift_y(x, k):
    pairs = []
    for d in range(DP):
        for s in range(SEQ):
            y = (s % YH) * YL + d // (XN * CORES)
            to = (y + k) % (YL * YH)
            d_to = (to % YL) * XN * CORES + d % (XN * CORES)
            pairs.append((d * SEQ + s, d_to * SEQ + (s // YH) * YH + to // YL))
    return lax.ppermute(x, ("dp", "seq"), pairs)


def spread(x, axis, n, groups=None):
    copies = jnp.broadcast_to(x[None], (n, *x.shape))
    return lax.all_to_all(copies, axis, 0, 0, tiled=True, axis_index_groups=groups)


def attend(nblk, order_ref, list_ref, count_ref, *refs):
    blocks = refs[:nblk]
    w_ref, cot_ref, att_ref, dqkv_ref, kv_rows, kv_cols, q_cols, acc = refs[nblk:]
    scale = HEAD_DIM ** (-0.5)
    tiles = kv_rows.shape[0]
    w = w_ref[...]
    w = jnp.concatenate([w[HEAD_DIM:], w[:HEAD_DIM]], axis=0)
    slot = 0
    for blk in blocks:
        qkv = dot(blk[...], w, 1, 1).astype(BF)
        for r in range(blk.shape[0] // TILE):
            tile = order_ref[slot]
            slot += 1
            piece = qkv[r * TILE : (r + 1) * TILE]
            kv = piece[:, :TILE]
            kv_rows[tile] = kv
            kv_cols[tile] = kv.T
            q_cols[tile] = piece[:, TILE:].T
    acc[...] = jnp.zeros_like(acc)
    zero = jnp.zeros((HEAD_DIM, TILE), BF)

    def step(a, _):
        left = jnp.concatenate([q_cols[a], zero], axis=0)
        right = jnp.concatenate([zero, cot_ref[a]], axis=0)
        both = jnp.concatenate([left, right], axis=1)
        keys = [list_ref[a, t] for t in range(TOP)]
        count = count_ref[a]
        rows = jnp.concatenate([kv_rows[j] for j in keys], axis=0)
        prod = dot(rows, both, 1, 0)
        raw = prod[:, :TILE]
        dprobs = prod[:, TILE:]
        parts = [raw[t * TILE : (t + 1) * TILE] for t in range(TOP)]
        raw = jnp.concatenate(
            parts[:1] + [jnp.where(t < count, parts[t], -1e30) for t in range(1, TOP)], axis=0
        )
        top = jnp.max(raw, axis=0, keepdims=True)
        expo = jnp.exp((raw - top) * scale)
        probs = expo * (1.0 / jnp.sum(expo, axis=0, keepdims=True))
        delta = jnp.sum(probs * dprobs, axis=0, keepdims=True)
        dscores = (probs * ((dprobs - delta) * scale)).astype(BF)
        pair = jnp.concatenate([dscores, probs.astype(BF)], axis=1)
        cols = jnp.concatenate([kv_cols[j] for j in keys], axis=1)
        out = dot(cols, pair, 1, 0)
        dqkv_ref[a, :HEAD_DIM, :] = out[:HEAD_DIM, :TILE].astype(BF)
        att_ref[a] = out[HEAD_DIM:, TILE:].astype(BF)
        both_t = jnp.concatenate([left.T, right.T], axis=0)
        back = dot(pair, both_t, 1, 0)
        for t in range(TOP):
            acc[keys[t]] += back[t * TILE : (t + 1) * TILE]
        return 0

    lax.fori_loop(0, tiles, step, 0, unroll=2)
    for a in range(tiles):
        dqkv_ref[a, HEAD_DIM:, :] = acc[a].astype(BF).T


def attention(order, tile_list, counts, blocks, w_head, cot_t):
    tiles = tile_list.shape[0]
    return pl.pallas_call(
        functools.partial(attend, len(blocks)),
        out_shape=(
            jax.ShapeDtypeStruct((tiles, HEAD_DIM, TILE), BF),
            jax.ShapeDtypeStruct((tiles, 3 * HEAD_DIM, TILE), BF),
        ),
        in_specs=[SM, SM, SM] + [VM] * (len(blocks) + 2),
        out_specs=(VM, VM),
        scratch_shapes=[
            pltpu.VMEM((tiles, TILE, 2 * HEAD_DIM), BF),
            pltpu.VMEM((tiles, 2 * HEAD_DIM, TILE), BF),
            pltpu.VMEM((tiles, HEAD_DIM, TILE), BF),
            pltpu.VMEM((tiles, TILE, 2 * HEAD_DIM), F32),
        ],
        compiler_params=PARAMS,
        name="attend",
    )(order, tile_list, counts, *blocks, w_head, cot_t)


def weight_sum(nblk, order_ref, dqkv_ref, *refs):
    blocks, out_ref = refs[:nblk], refs[nblk]
    total, slot = None, 0
    for blk in blocks:
        n = blk.shape[0] // TILE
        left = jnp.concatenate([dqkv_ref[order_ref[slot + r]] for r in range(n)], axis=1)
        slot += n
        part = dot(left, blk[...], 1, 0)
        total = part if total is None else total + part
    owners, rows = out_ref.shape[:2]
    for i in range(owners):
        out_ref[i] = total[i * rows : (i + 1) * rows].astype(BF)


def weight_grad(order, dqkv_t, blocks, owners):
    rows, depth = dqkv_t.shape[1] // owners, blocks[0].shape[1]
    return pl.pallas_call(
        functools.partial(weight_sum, len(blocks)),
        out_shape=jax.ShapeDtypeStruct((owners, rows, depth), BF),
        in_specs=[SM, VM] + [VM] * len(blocks),
        out_specs=VM,
        compiler_params=PARAMS,
        name="weight_sum",
    )(order, dqkv_t, *blocks)


def input_sum(split, place_ref, dqkv_ref, *refs):
    weights, out_ref = refs[:-1], refs[-1]
    heads = dqkv_ref.shape[0]
    chunk = 3 * HEAD_DIM // XN
    cols = jnp.concatenate(
        [dqkv_ref[h, c * chunk : (c + 1) * chunk, :] for c in range(XN) for h in range(heads)],
        axis=0,
    )
    left = cols.T
    k = 0
    for p in range(YL):
        total, at = None, 0
        for _ in range(split[p]):
            mine, other = weights[2 * k][...], weights[2 * k + 1][...]
            k += 1
            depth = mine.shape[0] * mine.shape[1] * mine.shape[2]
            both = jnp.concatenate([mine.reshape(depth, TILE), other.reshape(depth, TILE)], axis=1)
            part = dot(left[:, at : at + depth], both, 1, 0)
            at += depth
            total = part if total is None else total + part
        for c in range(CORES):
            where = pl.multiple_of(place_ref[2 * p + c] * TILE, TILE)
            out_ref[:, pl.ds(where, TILE)] = total[:, c * TILE : (c + 1) * TILE].astype(BF)


def input_grad(place, dqkv_t, split, weights):
    return pl.pallas_call(
        functools.partial(input_sum, split),
        out_shape=jax.ShapeDtypeStruct((TILE, YL * CORES * TILE), BF),
        in_specs=[SM, VM] + [VM] * len(weights),
        out_specs=VM,
        compiler_params=PARAMS,
        name="input_sum",
    )(place, dqkv_t, *weights)


def shards(tokens, qkv_weight, key_tiles, key_counts, cotangent):
    heads = SEQ
    depth = tokens.shape[2]
    tiles = key_tiles.shape[1]
    dp, seq = lax.axis_index("dp"), lax.axis_index("seq")
    y_lo, x, core = dp // (XN * CORES), dp // CORES % XN, dp % CORES
    z, y_hi = seq // YH, seq % YH
    grad_scale = (DP * tiles * TILE) ** (-0.5)

    w_head = spread(qkv_weight[0], "dp", DP).reshape(3 * HEAD_DIM, depth)
    chunk = 3 * HEAD_DIM // XN
    w_block = lax.dynamic_slice(
        w_head, (x * chunk, (y_lo * CORES + core) * TILE), (chunk, TILE)
    )

    own = tokens[0]
    pair = jnp.concatenate([own, flip_y(own)], axis=0)
    right, left = [pair], [pair]
    for _ in range(ZN // 2 - 1):
        right.append(shift_z(right[-1], 1))
        left.append(shift_z(left[-1], -1))
    far = [shift_z(right[-1][:TILE], 1), shift_z(left[-1][TILE:], -1)]
    blocks = right + left[1:] + far
    zs = [(0, 0), (0, 1)]
    zs += [(-k, j) for k in range(1, ZN // 2) for j in range(2)]
    zs += [(k, j) for k in range(1, ZN // 2) for j in range(2)]
    zs += [(ZN // 2, 0), (ZN // 2, 1)]
    order = jnp.stack([(z + k) % ZN * YH + (y_hi + j) % YH for k, j in zs]).astype(jnp.int32)

    cot_t = cotangent[0].T.reshape(heads, HEAD_DIM, TILE)
    cot_t = lax.all_to_all(cot_t, "seq", 0, 0, tiled=True)

    w_seq = spread(w_block, "seq", SEQ)
    x_groups = [
        [(y * XN + i) * CORES + c for i in range(XN)] for y in range(YL) for c in range(CORES)
    ]
    w_0 = spread(w_seq, "dp", XN, x_groups)
    w_m, w_p = shift_y(w_0, 1), shift_y(w_0, -1)
    half = XN // 2
    w_f = [shift_y(w_m[:half], 1), shift_y(w_p[half:], -1)]
    pieces = [w_0, w_m, w_p, *w_f]
    weights = []
    for piece in pieces:
        weights += [piece, swap_core(piece)]
    place = jnp.stack(
        [
            (y_lo + k) % YL * CORES + (core + c) % CORES
            for k in (0, YL - 1, 1, 2)
            for c in range(CORES)
        ]
    ).astype(jnp.int32)

    att_t, dqkv_t = attention(order, key_tiles[0], key_counts[0], blocks, w_head, cot_t)
    token_grads = lax.all_to_all(dqkv_t, "seq", 0, 0, tiled=True)
    att_t = lax.all_to_all(att_t, "seq", 0, 0, tiled=True)
    attended = att_t.reshape(heads * HEAD_DIM, TILE).T[None]

    parts = weight_grad(order, dqkv_t, blocks, DP)
    parts = lax.all_to_all(parts, "dp", 0, 0, tiled=True)
    grad_weight = jnp.sum(parts.astype(F32), axis=0)[None] * grad_scale

    grad_input = input_grad(place, token_grads, (1, 1, 1, 2), weights)[None]
    return (attended, grad_input, grad_weight)


def solution(mesh):
    in_specs = (
        P("dp", "seq", None),
        P("seq", "dp", None),
        P("dp", None, None),
        P("dp", None),
        P("dp", "seq", None),
    )
    out_specs = (P("dp", "seq", None), P("dp", "seq", None), P("seq", "dp", None))
    return jax.shard_map(shards, mesh=mesh, in_specs=in_specs, out_specs=out_specs, check_vma=False)
```

```python
import functools

import jax
import jax.numpy as jnp
from jax import lax
from jax.experimental import pallas as pl
from jax.experimental.pallas import tpu as pltpu
from jax.sharding import PartitionSpec as P

HEAD_DIM = 64
TILE = 128
TOP = 4
BF = jnp.bfloat16
F32 = jnp.float32
VM = pl.BlockSpec(memory_space=pltpu.VMEM)
SM = pl.BlockSpec(memory_space=pltpu.SMEM)
PARAMS = pltpu.CompilerParams(vmem_limit_bytes=48 * 2**20)

YL, XN, CORES, ZN, YH = 4, 4, 2, 8, 2
DP = YL * XN * CORES
SEQ = ZN * YH


def dot(a, b, ca, cb):
    return lax.dot_general(a, b, (((ca,), (cb,)), ((), ())), preferred_element_type=F32)


def flip_y(x):
    return lax.ppermute(x, "seq", [(s, s ^ 1) for s in range(SEQ)])


def shift_z(x, k):
    return lax.ppermute(x, "seq", [(s, (s + YH * k) % SEQ) for s in range(SEQ)])


def swap_core(x):
    return lax.ppermute(x, "dp", [(d, d ^ 1) for d in range(DP)])


def shift_x(x, k):
    pairs = []
    for d in range(DP):
        to = (d // CORES + k) % XN
        pairs.append((d, d // (XN * CORES) * XN * CORES + to * CORES + d % CORES))
    return lax.ppermute(x, "dp", pairs)


def shift_y(x, k):
    return lax.ppermute(x, "dp", [(d, (d + k * XN * CORES) % DP) for d in range(DP)])


def spread(x, axis, n):
    copies = jnp.broadcast_to(x[None], (n, *x.shape))
    return lax.all_to_all(copies, axis, 0, 0, tiled=True)


def attend(nblk, order_ref, list_ref, count_ref, *refs):
    blocks = refs[:nblk]
    w_ref, cot_ref, out_ref, kv_rows, kv_cols, q_cols, acc = refs[nblk:]
    scale = HEAD_DIM ** (-0.5)
    tiles = kv_rows.shape[0]
    w = w_ref[...]
    w = jnp.concatenate([w[HEAD_DIM:], w[:HEAD_DIM]], axis=0)
    slot = 0
    for blk in blocks:
        qkv = dot(blk[...], w, 1, 1).astype(BF)
        for r in range(blk.shape[0] // TILE):
            tile = order_ref[slot]
            slot += 1
            piece = qkv[r * TILE : (r + 1) * TILE]
            kv = piece[:, :TILE]
            kv_rows[tile] = kv
            kv_cols[tile] = kv.T
            q_cols[tile] = piece[:, TILE:].T
    acc[...] = jnp.zeros_like(acc)
    zero = jnp.zeros((HEAD_DIM, TILE), BF)

    def step(a, _):
        left = jnp.concatenate([q_cols[a], zero], axis=0)
        right = jnp.concatenate([zero, cot_ref[a, :HEAD_DIM, :]], axis=0)
        both = jnp.concatenate([left, right], axis=1)
        keys = [list_ref[a, t] for t in range(TOP)]
        count = count_ref[a]
        rows = jnp.concatenate([kv_rows[j] for j in keys], axis=0)
        prod = dot(rows, both, 1, 0)
        raw = prod[:, :TILE]
        dprobs = prod[:, TILE:]
        parts = [raw[t * TILE : (t + 1) * TILE] for t in range(TOP)]
        raw = jnp.concatenate(
            parts[:1] + [jnp.where(t < count, parts[t], -1e30) for t in range(1, TOP)], axis=0
        )
        top = jnp.max(raw, axis=0, keepdims=True)
        expo = jnp.exp((raw - top) * scale)
        probs = expo * (1.0 / jnp.sum(expo, axis=0, keepdims=True))
        delta = jnp.sum(probs * dprobs, axis=0, keepdims=True)
        dscores = (probs * ((dprobs - delta) * scale)).astype(BF)
        pair = jnp.concatenate([dscores, probs.astype(BF)], axis=1)
        cols = jnp.concatenate([kv_cols[j] for j in keys], axis=1)
        out = dot(cols, pair, 1, 0)
        out_ref[a, :HEAD_DIM, :] = out[:HEAD_DIM, :TILE].astype(BF)
        out_ref[a, 3 * HEAD_DIM :, :] = out[HEAD_DIM:, TILE:].astype(BF)
        both_t = jnp.concatenate([left.T, right.T], axis=0)
        back = dot(pair, both_t, 1, 0)
        for t in range(TOP):
            acc[keys[t]] += back[t * TILE : (t + 1) * TILE]
        return 0

    lax.fori_loop(0, tiles, step, 0, unroll=2)
    for a in range(tiles):
        out_ref[a, HEAD_DIM : 3 * HEAD_DIM, :] = acc[a].astype(BF).T


def attention(order, tile_list, counts, blocks, w_head, cot_t):
    tiles = tile_list.shape[0]
    return pl.pallas_call(
        functools.partial(attend, len(blocks)),
        out_shape=jax.ShapeDtypeStruct((tiles, 4 * HEAD_DIM, TILE), BF),
        in_specs=[SM, SM, SM] + [VM] * (len(blocks) + 2),
        out_specs=VM,
        scratch_shapes=[
            pltpu.VMEM((tiles, TILE, 2 * HEAD_DIM), BF),
            pltpu.VMEM((tiles, 2 * HEAD_DIM, TILE), BF),
            pltpu.VMEM((tiles, HEAD_DIM, TILE), BF),
            pltpu.VMEM((tiles, TILE, 2 * HEAD_DIM), F32),
        ],
        compiler_params=PARAMS,
        name="attend",
    )(order, tile_list, counts, *blocks, w_head, cot_t)


def weight_sum(nblk, here_ref, order_ref, dqkv_ref, *refs):
    blocks, out_ref = refs[:nblk], refs[nblk]
    total, slot = None, 0
    for blk in blocks:
        n = blk.shape[0] // TILE
        left = [dqkv_ref[order_ref[slot + r], : 3 * HEAD_DIM, :] for r in range(n)]
        slot += n
        part = dot(jnp.concatenate(left, axis=1), blk[...], 1, 0)
        total = part if total is None else total + part
    rows = out_ref.shape[3]
    core, x, y = here_ref[0], here_ref[1], here_ref[2]
    for i in range(DP):
        c = lax.rem(i % CORES + CORES - core, CORES)
        u = lax.rem(i // CORES % XN + XN - x, XN)
        v = lax.rem(i // (CORES * XN) + YL - y, YL)
        out_ref[c, u, v] = total[i * rows : (i + 1) * rows]


def weight_grad(here, order, dqkv_t, blocks):
    rows, depth = 3 * HEAD_DIM // DP, blocks[0].shape[1]
    return pl.pallas_call(
        functools.partial(weight_sum, len(blocks)),
        out_shape=jax.ShapeDtypeStruct((CORES, XN, YL, rows, depth), F32),
        in_specs=[SM, SM, VM] + [VM] * len(blocks),
        out_specs=VM,
        compiler_params=PARAMS,
        name="weight_sum",
    )(here, order, dqkv_t, *blocks)


def input_sum(both_ref, w_ref, att_ref, out_ref):
    heads = both_ref.shape[0]
    chunk = 3 * HEAD_DIM // XN
    att_ref[...] = jnp.concatenate(
        [both_ref[h, 3 * HEAD_DIM :, :] for h in range(heads)], axis=0
    ).T
    left = jnp.concatenate(
        [both_ref[h, c * chunk : (c + 1) * chunk, :] for c in range(XN) for h in range(heads)],
        axis=0,
    ).T
    for y in range(YL):
        cols = []
        for c in range(CORES):
            part = [w_ref[(y * XN + u) * CORES + c] for u in range(XN)]
            cols.append(jnp.concatenate([p.reshape(heads * chunk, TILE) for p in part], axis=0))
        total = dot(left, jnp.concatenate(cols, axis=1), 1, 0)
        at = y * CORES * TILE
        out_ref[:, at : at + CORES * TILE] = total.astype(BF)


def input_grad(both, w_all):
    heads = both.shape[0]
    return pl.pallas_call(
        input_sum,
        out_shape=(
            jax.ShapeDtypeStruct((TILE, heads * HEAD_DIM), BF),
            jax.ShapeDtypeStruct((TILE, YL * CORES * TILE), BF),
        ),
        in_specs=[VM, VM],
        out_specs=(VM, VM),
        compiler_params=PARAMS,
        name="input_sum",
    )(both, w_all)


def shards(tokens, qkv_weight, key_tiles, key_counts, cotangent):
    heads = SEQ
    depth = tokens.shape[2]
    tiles = key_tiles.shape[1]
    dp, seq = lax.axis_index("dp"), lax.axis_index("seq")
    y_lo, x, core = dp // (XN * CORES), dp // CORES % XN, dp % CORES
    z, y_hi = seq // YH, seq % YH
    grad_scale = (DP * tiles * TILE) ** (-0.5)

    w_head = spread(qkv_weight[0], "dp", DP).reshape(3 * HEAD_DIM, depth)
    chunk = 3 * HEAD_DIM // XN
    w_block = lax.dynamic_slice(
        w_head, (x * chunk, (y_lo * CORES + core) * TILE), (chunk, TILE)
    )

    own = tokens[0]
    pair = jnp.concatenate([own, flip_y(own)], axis=0)
    right, left = [pair], [pair]
    for _ in range(ZN // 2 - 1):
        right.append(shift_z(right[-1], 1))
        left.append(shift_z(left[-1], -1))
    far = [shift_z(right[-1][:TILE], 1), shift_z(left[-1][TILE:], -1)]
    blocks = right + left[1:] + far
    zs = [(0, 0), (0, 1)]
    zs += [(-k, j) for k in range(1, ZN // 2) for j in range(2)]
    zs += [(k, j) for k in range(1, ZN // 2) for j in range(2)]
    zs += [(ZN // 2, 0), (ZN // 2, 1)]
    order = jnp.stack([(z + k) % ZN * YH + (y_hi + j) % YH for k, j in zs]).astype(jnp.int32)

    cot_t = cotangent[0].T.reshape(heads, HEAD_DIM, TILE)
    copies = jnp.broadcast_to(w_block[None], (heads, *w_block.shape))
    mixed = jnp.concatenate([cot_t, copies], axis=1)
    mixed, _ = lax.optimization_barrier((mixed, pair))
    mixed = lax.all_to_all(mixed, "seq", 0, 0, tiled=True)
    w_seq, _ = lax.optimization_barrier((mixed[:, HEAD_DIM:], (right[1], left[1])))
    w_all = lax.all_gather(w_seq, "dp", axis=0)

    both = attention(order, key_tiles[0], key_counts[0], blocks, w_head, mixed)
    here = jnp.stack([core, x, y_lo]).astype(jnp.int32)
    sums = weight_grad(here, order, both, blocks)
    both = lax.all_to_all(both, "seq", 0, 0, tiled=True)

    sums = sums[0] + swap_core(sums[1])
    sums = sums[0] + sum(shift_x(sums[k], k) for k in range(1, XN))
    sums = sums[0] + sum(shift_y(sums[k], k) for k in range(1, YL))
    grad_weight = sums[None] * grad_scale

    attended, grad_input = input_grad(both, w_all)
    return (attended[None], grad_input[None], grad_weight)


def solution(mesh):
    in_specs = (
        P("dp", "seq", None),
        P("seq", "dp", None),
        P("dp", None, None),
        P("dp", None),
        P("dp", "seq", None),
    )
    out_specs = (P("dp", "seq", None), P("dp", "seq", None), P("seq", "dp", None))
    return jax.shard_map(shards, mesh=mesh, in_specs=in_specs, out_specs=out_specs, check_vma=False)
```

```python
import functools

import jax
import jax.numpy as jnp
from jax import lax
from jax.experimental import pallas as pl
from jax.experimental.pallas import tpu as pltpu
from jax.sharding import PartitionSpec as P

HEAD_DIM = 64
TILE = 128
TOP = 4
BF = jnp.bfloat16
F32 = jnp.float32
VM = pl.BlockSpec(memory_space=pltpu.VMEM)
SM = pl.BlockSpec(memory_space=pltpu.SMEM)
PARAMS = pltpu.CompilerParams(vmem_limit_bytes=48 * 2**20)

YL, XN, CORES, ZN, YH = 4, 4, 2, 8, 2
DP = YL * XN * CORES
SEQ = ZN * YH


def dot(a, b, ca, cb):
    return lax.dot_general(a, b, (((ca,), (cb,)), ((), ())), preferred_element_type=F32)


def flip_y(x):
    return lax.ppermute(x, "seq", [(s, s ^ 1) for s in range(SEQ)])


def shift_z(x, k):
    return lax.ppermute(x, "seq", [(s, (s + YH * k) % SEQ) for s in range(SEQ)])


def swap_core(x):
    return lax.ppermute(x, "dp", [(d, d ^ 1) for d in range(DP)])


def shift_x(x, k):
    pairs = []
    for d in range(DP):
        to = (d // CORES + k) % XN
        pairs.append((d, d // (XN * CORES) * XN * CORES + to * CORES + d % CORES))
    return lax.ppermute(x, "dp", pairs)


def shift_y(x, k):
    return lax.ppermute(x, "dp", [(d, (d + k * XN * CORES) % DP) for d in range(DP)])


def spread(x, axis, n):
    copies = jnp.broadcast_to(x[None], (n, *x.shape))
    return lax.all_to_all(copies, axis, 0, 0, tiled=True)


def tiles_of(blocks):
    own, flip, r1, l1, r2, r3, l2, l3, r4, l4, r5, l5 = blocks
    half = TILE // 2
    yield from (own[...], flip[...], r1[...], l1[...])
    for pair in (r2, r3, l2, l3):
        yield pair[...]
    yield r4[:TILE]
    yield l4[half:]
    yield jnp.concatenate([r4[TILE:], l4[:half]], axis=0)
    yield jnp.concatenate([r5[...], l5[...]], axis=0)


def tile_places(z, y_hi):
    steps = [(0, 0), (0, 1), (-1, 0), (1, 0), (-1, 1), (-2, 0), (-2, 1), (-3, 0)]
    steps += [(2, 0), (1, 1), (3, 0), (2, 1), (-3, 1), (3, 1), (4, 0), (4, 1)]
    places = [lax.rem(z + k + ZN, ZN) * YH + lax.rem(y_hi + j, YH) for k, j in steps]
    return jnp.stack(places).astype(jnp.int32)


def gather_scene(own):
    flip, r1, l1 = flip_y(own), shift_z(own, 1), shift_z(own, -1)
    r2 = shift_z(jnp.concatenate([flip, r1], axis=0), 1)
    l2 = shift_z(jnp.concatenate([l1, flip], axis=0), -1)
    r3, l3 = shift_z(r2, 1), shift_z(l2, -1)
    half = TILE // 2
    r4, l4 = shift_z(r3[: TILE + half], 1), shift_z(l3[half:], -1)
    r5, l5 = shift_z(r4[:half], 1), shift_z(l4[TILE:], -1)
    return own, flip, r1, l1, r2, r3, l2, l3, r4, l4, r5, l5


def attend(nblk, here_ref, order_ref, list_ref, count_ref, *refs):
    blocks = refs[:nblk]
    w_ref, cot_ref, out_ref, sum_ref, kv_rows, kv_cols, q_cols, acc = refs[nblk:]
    scale = HEAD_DIM ** (-0.5)
    tiles = kv_rows.shape[0]
    w = w_ref[...]
    w = jnp.concatenate([w[HEAD_DIM:], w[:HEAD_DIM]], axis=0)
    slot = 0
    for blk in tiles_of(blocks):
        qkv = dot(blk, w, 1, 1).astype(BF)
        for r in range(blk.shape[0] // TILE):
            tile = order_ref[slot]
            slot += 1
            piece = qkv[r * TILE : (r + 1) * TILE]
            kv = piece[:, :TILE]
            kv_rows[tile] = kv
            kv_cols[tile] = kv.T
            q_cols[tile] = piece[:, TILE:].T
    acc[...] = jnp.zeros_like(acc)
    zero = jnp.zeros((HEAD_DIM, TILE), BF)

    def step(a, _):
        left = jnp.concatenate([q_cols[a], zero], axis=0)
        right = jnp.concatenate([zero, cot_ref[a, :HEAD_DIM, :]], axis=0)
        both = jnp.concatenate([left, right], axis=1)
        keys = [list_ref[a, t] for t in range(TOP)]
        count = count_ref[a]
        rows = jnp.concatenate([kv_rows[j] for j in keys], axis=0)
        prod = dot(rows, both, 1, 0)
        raw = prod[:, :TILE]
        dprobs = prod[:, TILE:]
        parts = [raw[t * TILE : (t + 1) * TILE] for t in range(TOP)]
        raw = jnp.concatenate(
            parts[:1] + [jnp.where(t < count, parts[t], -1e30) for t in range(1, TOP)], axis=0
        )
        top = jnp.max(raw, axis=0, keepdims=True)
        expo = jnp.exp((raw - top) * scale)
        probs = expo * (1.0 / jnp.sum(expo, axis=0, keepdims=True))
        delta = jnp.sum(probs * dprobs, axis=0, keepdims=True)
        dscores = (probs * ((dprobs - delta) * scale)).astype(BF)
        pair = jnp.concatenate([dscores, probs.astype(BF)], axis=1)
        cols = jnp.concatenate([kv_cols[j] for j in keys], axis=1)
        out = dot(cols, pair, 1, 0)
        out_ref[a, :HEAD_DIM, :] = out[:HEAD_DIM, :TILE].astype(BF)
        out_ref[a, 3 * HEAD_DIM :, :] = out[HEAD_DIM:, TILE:].astype(BF)
        both_t = jnp.concatenate([left.T, right.T], axis=0)
        back = dot(pair, both_t, 1, 0)
        for t in range(TOP):
            acc[keys[t]] += back[t * TILE : (t + 1) * TILE]
        return 0

    lax.fori_loop(0, tiles, step, 0, unroll=2)
    for a in range(tiles):
        out_ref[a, HEAD_DIM : 3 * HEAD_DIM, :] = acc[a].astype(BF).T

    total, slot = None, 0
    for blk in tiles_of(blocks):
        n = blk.shape[0] // TILE
        left = [out_ref[order_ref[slot + r], : 3 * HEAD_DIM, :] for r in range(n)]
        slot += n
        part = dot(jnp.concatenate(left, axis=1), blk, 1, 0)
        total = part if total is None else total + part
    rows = sum_ref.shape[3]
    core, x, y = here_ref[0], here_ref[1], here_ref[2]
    for i in range(DP):
        c = lax.rem(i % CORES + CORES - core, CORES)
        u = lax.rem(i // CORES % XN + XN - x, XN)
        v = lax.rem(i // (CORES * XN) + YL - y, YL)
        sum_ref[c, u, v] = total[i * rows : (i + 1) * rows]


def attention(here, order, tile_list, counts, blocks, w_head, cot_t):
    tiles = tile_list.shape[0]
    rows, depth = w_head.shape[0] // DP, w_head.shape[1]
    return pl.pallas_call(
        functools.partial(attend, len(blocks)),
        out_shape=(
            jax.ShapeDtypeStruct((tiles, 4 * HEAD_DIM, TILE), BF),
            jax.ShapeDtypeStruct((CORES, XN, YL, rows, depth), F32),
        ),
        in_specs=[SM, SM, SM, SM] + [VM] * (len(blocks) + 2),
        out_specs=(VM, VM),
        scratch_shapes=[
            pltpu.VMEM((tiles, TILE, 2 * HEAD_DIM), BF),
            pltpu.VMEM((tiles, 2 * HEAD_DIM, TILE), BF),
            pltpu.VMEM((tiles, HEAD_DIM, TILE), BF),
            pltpu.VMEM((tiles, TILE, 2 * HEAD_DIM), F32),
        ],
        compiler_params=PARAMS,
        name="attend",
    )(here, order, tile_list, counts, *blocks, w_head, cot_t)


def input_sum(both_ref, w_ref, att_ref, out_ref):
    heads = both_ref.shape[0]
    chunk = 3 * HEAD_DIM // XN
    att_ref[...] = jnp.concatenate(
        [both_ref[h, 3 * HEAD_DIM :, :] for h in range(heads)], axis=0
    ).T
    left = jnp.concatenate(
        [both_ref[h, c * chunk : (c + 1) * chunk, :] for c in range(XN) for h in range(heads)],
        axis=0,
    ).T
    for y in range(YL):
        cols = []
        for c in range(CORES):
            part = [w_ref[(y * XN + u) * CORES + c] for u in range(XN)]
            cols.append(jnp.concatenate([p.reshape(heads * chunk, TILE) for p in part], axis=0))
        total = dot(left, jnp.concatenate(cols, axis=1), 1, 0)
        at = y * CORES * TILE
        out_ref[:, at : at + CORES * TILE] = total.astype(BF)


def input_grad(both, w_all):
    heads = both.shape[0]
    return pl.pallas_call(
        input_sum,
        out_shape=(
            jax.ShapeDtypeStruct((TILE, heads * HEAD_DIM), BF),
            jax.ShapeDtypeStruct((TILE, YL * CORES * TILE), BF),
        ),
        in_specs=[VM, VM],
        out_specs=(VM, VM),
        compiler_params=PARAMS,
        name="input_sum",
    )(both, w_all)


def shards(tokens, qkv_weight, key_tiles, key_counts, cotangent):
    heads = SEQ
    depth = tokens.shape[2]
    tiles = key_tiles.shape[1]
    dp, seq = lax.axis_index("dp"), lax.axis_index("seq")
    y_lo, x, core = dp // (XN * CORES), dp // CORES % XN, dp % CORES
    z, y_hi = seq // YH, seq % YH
    grad_scale = (DP * tiles * TILE) ** (-0.5)

    blocks = gather_scene(tokens[0])
    flip, r1, l1, r2, r3, l2, l3 = blocks[1:8]

    w_own, _ = lax.optimization_barrier((qkv_weight[0], (flip, r1, l1)))
    w_head = spread(w_own, "dp", DP).reshape(3 * HEAD_DIM, depth)
    chunk = 3 * HEAD_DIM // XN
    w_block = lax.dynamic_slice(
        w_head, (x * chunk, (y_lo * CORES + core) * TILE), (chunk, TILE)
    )

    cot_t = cotangent[0].T.reshape(heads, HEAD_DIM, TILE)
    copies = jnp.broadcast_to(w_block[None], (heads, *w_block.shape))
    mixed = jnp.concatenate([cot_t, copies], axis=1)
    mixed, _ = lax.optimization_barrier((mixed, (r2, l2)))
    mixed = lax.all_to_all(mixed, "seq", 0, 0, tiled=True)
    w_seq, _ = lax.optimization_barrier((mixed[:, HEAD_DIM:], (r3, l3)))
    w_all = lax.all_gather(w_seq, "dp", axis=0)

    here = jnp.stack([core, x, y_lo]).astype(jnp.int32)
    order = tile_places(z, y_hi)
    both, sums = attention(here, order, key_tiles[0], key_counts[0], blocks, w_head, mixed)
    both = lax.all_to_all(both, "seq", 0, 0, tiled=True)

    sums = sums[0] + swap_core(sums[1])
    sums = sums[0] + sum(shift_x(sums[k], k) for k in range(1, XN))
    sums = sums[0] + sum(shift_y(sums[k], k) for k in range(1, YL))
    grad_weight = sums[None] * grad_scale

    attended, grad_input = input_grad(both, w_all)
    return (attended[None], grad_input[None], grad_weight)


def solution(mesh):
    in_specs = (
        P("dp", "seq", None),
        P("seq", "dp", None),
        P("dp", None, None),
        P("dp", None),
        P("dp", "seq", None),
    )
    out_specs = (P("dp", "seq", None), P("dp", "seq", None), P("seq", "dp", None))
    return jax.shard_map(shards, mesh=mesh, in_specs=in_specs, out_specs=out_specs, check_vma=False)
```

```python
import functools

import jax
import jax.numpy as jnp
from jax import lax
from jax.experimental import pallas as pl
from jax.experimental.pallas import tpu as pltpu
from jax.sharding import PartitionSpec as P

HEAD_DIM = 64
TILE = 128
TOP = 4
BF = jnp.bfloat16
F32 = jnp.float32
VM = pl.BlockSpec(memory_space=pltpu.VMEM)
SM = pl.BlockSpec(memory_space=pltpu.SMEM)
PARAMS = pltpu.CompilerParams(vmem_limit_bytes=48 * 2**20)

YL, XN, CORES, ZN, YH = 4, 4, 2, 8, 2
DP = YL * XN * CORES
SEQ = ZN * YH


def dot(a, b, ca, cb):
    return lax.dot_general(a, b, (((ca,), (cb,)), ((), ())), preferred_element_type=F32)


def flip_y(x):
    return lax.ppermute(x, "seq", [(s, s ^ 1) for s in range(SEQ)])


def shift_z(x, k):
    return lax.ppermute(x, "seq", [(s, (s + YH * k) % SEQ) for s in range(SEQ)])


def swap_dp(x, bit):
    return lax.ppermute(x, "dp", [(d, d ^ bit) for d in range(DP)])


def spread(x, axis, n):
    copies = jnp.broadcast_to(x[None], (n, *x.shape))
    return lax.all_to_all(copies, axis, 0, 0, tiled=True)


def mirror(dp):
    return sum(((dp >> k) & 1) << (4 - k) for k in range(5))


def tiles_of(blocks):
    own, flip, r1, l1, r2, r3, l2, l3, r4, l4, r5, l5 = blocks
    half = TILE // 2
    yield from (own[...], flip[...], r1[...], l1[...])
    for pair in (r2, r3, l2, l3):
        yield pair[...]
    yield r4[:TILE]
    yield l4[half:]
    yield jnp.concatenate([r4[TILE:], l4[:half]], axis=0)
    yield jnp.concatenate([r5[...], l5[...]], axis=0)


def tile_places(z, y_hi):
    steps = [(0, 0), (0, 1), (-1, 0), (1, 0), (-1, 1), (-2, 0), (-2, 1), (-3, 0)]
    steps += [(2, 0), (1, 1), (3, 0), (2, 1), (-3, 1), (3, 1), (4, 0), (4, 1)]
    places = [lax.rem(z + k + ZN, ZN) * YH + lax.rem(y_hi + j, YH) for k, j in steps]
    return jnp.stack(places).astype(jnp.int32)


def gather_scene(own):
    flip, r1, l1 = flip_y(own), shift_z(own, 1), shift_z(own, -1)
    r2 = shift_z(jnp.concatenate([flip, r1], axis=0), 1)
    l2 = shift_z(jnp.concatenate([l1, flip], axis=0), -1)
    r3, l3 = shift_z(r2, 1), shift_z(l2, -1)
    half = TILE // 2
    r4, l4 = shift_z(r3[: TILE + half], 1), shift_z(l3[half:], -1)
    r5, l5 = shift_z(r4[:half], 1), shift_z(l4[TILE:], -1)
    return own, flip, r1, l1, r2, r3, l2, l3, r4, l4, r5, l5


def attend(nblk, here_ref, order_ref, list_ref, count_ref, *refs):
    blocks = refs[:nblk]
    w_ref, cot_ref, out_ref, sum_ref, kv_rows, kv_cols, q_cols, acc = refs[nblk:]
    scale = HEAD_DIM ** (-0.5)
    tiles = kv_rows.shape[0]
    w = w_ref[...]
    w = jnp.concatenate([w[HEAD_DIM:], w[:HEAD_DIM]], axis=0)
    slot = 0
    for blk in tiles_of(blocks):
        qkv = dot(blk, w, 1, 1).astype(BF)
        for r in range(blk.shape[0] // TILE):
            tile = order_ref[slot]
            slot += 1
            piece = qkv[r * TILE : (r + 1) * TILE]
            kv = piece[:, :TILE]
            kv_rows[tile] = kv
            kv_cols[tile] = kv.T
            q_cols[tile] = piece[:, TILE:].T
    acc[...] = jnp.zeros_like(acc)
    zero = jnp.zeros((HEAD_DIM, TILE), BF)

    def step(a, _):
        left = jnp.concatenate([q_cols[a], zero], axis=0)
        right = jnp.concatenate([zero, cot_ref[a, :HEAD_DIM, :]], axis=0)
        both = jnp.concatenate([left, right], axis=1)
        keys = [list_ref[a, t] for t in range(TOP)]
        count = count_ref[a]
        rows = jnp.concatenate([kv_rows[j] for j in keys], axis=0)
        prod = dot(rows, both, 1, 0)
        raw = prod[:, :TILE]
        dprobs = prod[:, TILE:]
        parts = [raw[t * TILE : (t + 1) * TILE] for t in range(TOP)]
        raw = jnp.concatenate(
            parts[:1] + [jnp.where(t < count, parts[t], -1e30) for t in range(1, TOP)], axis=0
        )
        top = jnp.max(raw, axis=0, keepdims=True)
        expo = jnp.exp((raw - top) * scale)
        probs = expo * (1.0 / jnp.sum(expo, axis=0, keepdims=True))
        delta = jnp.sum(probs * dprobs, axis=0, keepdims=True)
        dscores = (probs * ((dprobs - delta) * scale)).astype(BF)
        pair = jnp.concatenate([dscores, probs.astype(BF)], axis=1)
        cols = jnp.concatenate([kv_cols[j] for j in keys], axis=1)
        out = dot(cols, pair, 1, 0)
        out_ref[a, :HEAD_DIM, :] = out[:HEAD_DIM, :TILE].astype(BF)
        out_ref[a, 3 * HEAD_DIM :, :] = out[HEAD_DIM:, TILE:].astype(BF)
        both_t = jnp.concatenate([left.T, right.T], axis=0)
        back = dot(pair, both_t, 1, 0)
        for t in range(TOP):
            acc[keys[t]] += back[t * TILE : (t + 1) * TILE]
        return 0

    lax.fori_loop(0, tiles, step, 0, unroll=2)
    for a in range(tiles):
        out_ref[a, HEAD_DIM : 3 * HEAD_DIM, :] = acc[a].astype(BF).T

    total, slot = None, 0
    for blk in tiles_of(blocks):
        n = blk.shape[0] // TILE
        left = [out_ref[order_ref[slot + r], : 3 * HEAD_DIM, :] for r in range(n)]
        slot += n
        part = dot(jnp.concatenate(left, axis=1), blk, 1, 0)
        total = part if total is None else total + part
    rows = sum_ref.shape[1]
    here = here_ref[0]
    for i in range(DP):
        sum_ref[mirror(i) ^ here] = total[i * rows : (i + 1) * rows]


def attention(here, order, tile_list, counts, blocks, w_head, cot_t):
    tiles = tile_list.shape[0]
    rows, depth = w_head.shape[0] // DP, w_head.shape[1]
    return pl.pallas_call(
        functools.partial(attend, len(blocks)),
        out_shape=(
            jax.ShapeDtypeStruct((tiles, 4 * HEAD_DIM, TILE), BF),
            jax.ShapeDtypeStruct((DP, rows, depth), F32),
        ),
        in_specs=[SM, SM, SM, SM] + [VM] * (len(blocks) + 2),
        out_specs=(VM, VM),
        scratch_shapes=[
            pltpu.VMEM((tiles, TILE, 2 * HEAD_DIM), BF),
            pltpu.VMEM((tiles, 2 * HEAD_DIM, TILE), BF),
            pltpu.VMEM((tiles, HEAD_DIM, TILE), BF),
            pltpu.VMEM((tiles, TILE, 2 * HEAD_DIM), F32),
        ],
        compiler_params=PARAMS,
        name="attend",
    )(here, order, tile_list, counts, *blocks, w_head, cot_t)


def input_sum(both_ref, w_ref, att_ref, out_ref, sorted_ref):
    heads = both_ref.shape[0]
    att_ref[...] = jnp.concatenate(
        [both_ref[h, 3 * HEAD_DIM :, :] for h in range(heads)], axis=0
    ).T
    rows = 3 * HEAD_DIM // DP
    for h in range(heads):
        part = both_ref[h, : 3 * HEAD_DIM, :].astype(F32)
        for d in range(DP):
            at = (d * heads + h) * rows
            sorted_ref[at : at + rows, :] = part[d * rows : (d + 1) * rows]
    left = sorted_ref[...].astype(BF).T
    out_ref[...] = dot(left, w_ref[...], 1, 0).astype(BF)


def input_grad(both, w_all):
    heads = both.shape[0]
    return pl.pallas_call(
        input_sum,
        out_shape=(
            jax.ShapeDtypeStruct((TILE, heads * HEAD_DIM), BF),
            jax.ShapeDtypeStruct((TILE, w_all.shape[1]), BF),
        ),
        in_specs=[VM, VM],
        out_specs=(VM, VM),
        scratch_shapes=[pltpu.VMEM((w_all.shape[0], TILE), F32)],
        compiler_params=PARAMS,
        name="input_sum",
    )(both, w_all)


def shards(tokens, qkv_weight, key_tiles, key_counts, cotangent):
    heads = SEQ
    depth = tokens.shape[2]
    tiles = key_tiles.shape[1]
    dp, seq = lax.axis_index("dp"), lax.axis_index("seq")
    z, y_hi = seq // YH, seq % YH
    grad_scale = (DP * tiles * TILE) ** (-0.5)

    blocks = gather_scene(tokens[0])

    own_rows = qkv_weight[0]
    rows = own_rows.shape[0]
    lanes = rows * depth // TILE
    cot_t = cotangent[0].T.reshape(heads, HEAD_DIM, TILE)
    copies = jnp.broadcast_to(own_rows.reshape(lanes, TILE)[None], (heads, lanes, TILE))
    mixed = jnp.concatenate([cot_t, copies], axis=1)
    mixed = lax.all_to_all(mixed, "seq", 0, 0, tiled=True)
    w_seq = mixed[:, HEAD_DIM:].reshape(heads * rows, depth)
    w_seq, _ = lax.optimization_barrier((w_seq, blocks[1:4]))
    w_all = lax.all_gather(w_seq, "dp", axis=0, tiled=True)

    own_rows, _ = lax.optimization_barrier((own_rows, mixed))
    w_head = spread(own_rows, "dp", DP).reshape(DP * rows, depth)

    here = mirror(dp)[None].astype(jnp.int32)
    order = tile_places(z, y_hi)
    both, sums = attention(here, order, key_tiles[0], key_counts[0], blocks, w_head, mixed)
    both = lax.all_to_all(both, "seq", 0, 0, tiled=True)

    for bit in (1, 2, 4, 8, 16):
        half = sums.shape[0] // 2
        sums = sums[:half] + swap_dp(sums[half:], bit)
    grad_weight = sums * grad_scale

    attended, grad_input = input_grad(both, w_all)
    return (attended[None], grad_input[None], grad_weight)


def solution(mesh):
    in_specs = (
        P("dp", "seq", None),
        P("seq", "dp", None),
        P("dp", None, None),
        P("dp", None),
        P("dp", "seq", None),
    )
    out_specs = (P("dp", "seq", None), P("dp", "seq", None), P("seq", "dp", None))
    return jax.shard_map(shards, mesh=mesh, in_specs=in_specs, out_specs=out_specs, check_vma=False)
```

```python
import functools

import jax
import jax.numpy as jnp
from jax import lax
from jax.experimental import pallas as pl
from jax.experimental.pallas import tpu as pltpu
from jax.sharding import PartitionSpec as P

HEAD_DIM = 64
TILE = 128
TOP = 4
BF = jnp.bfloat16
F32 = jnp.float32
VM = pl.BlockSpec(memory_space=pltpu.VMEM)
SM = pl.BlockSpec(memory_space=pltpu.SMEM)
PARAMS = pltpu.CompilerParams(vmem_limit_bytes=32 * 2**20)

YL, XN, CORES, ZN, YH = 4, 4, 2, 8, 2
DP = YL * XN * CORES
SEQ = ZN * YH


def dot(a, b, ca, cb):
    return lax.dot_general(a, b, (((ca,), (cb,)), ((), ())), preferred_element_type=F32)


def flip_y(x):
    return lax.ppermute(x, "seq", [(s, s ^ 1) for s in range(SEQ)])


def shift_z(x, k):
    return lax.ppermute(x, "seq", [(s, (s + YH * k) % SEQ) for s in range(SEQ)])


def swap_dp(x, bit):
    return lax.ppermute(x, "dp", [(d, d ^ bit) for d in range(DP)])


def spread(x, axis, n):
    copies = jnp.broadcast_to(x[None], (n, *x.shape))
    return lax.all_to_all(copies, axis, 0, 0, tiled=True)


def mirror(dp):
    return sum(((dp >> k) & 1) << (4 - k) for k in range(5))


def tiles_of(blocks):
    own, flip, r1, l1, r2, r3, l2, l3, r4, l4, r5, l5 = blocks
    half = TILE // 2
    yield from (own[...], flip[...], r1[...], l1[...])
    for pair in (r2, r3, l2, l3):
        yield pair[...]
    yield r4[:TILE]
    yield l4[half:]
    yield jnp.concatenate([r4[TILE:], l4[:half]], axis=0)
    yield jnp.concatenate([r5[...], l5[...]], axis=0)


def tile_places(z, y_hi):
    steps = [(0, 0), (0, 1), (-1, 0), (1, 0), (-1, 1), (-2, 0), (-2, 1), (-3, 0)]
    steps += [(2, 0), (1, 1), (3, 0), (2, 1), (-3, 1), (3, 1), (4, 0), (4, 1)]
    places = [lax.rem(z + k + ZN, ZN) * YH + lax.rem(y_hi + j, YH) for k, j in steps]
    return jnp.stack(places).astype(jnp.int32)


def gather_scene(own):
    flip, r1, l1 = flip_y(own), shift_z(own, 1), shift_z(own, -1)
    r2 = shift_z(jnp.concatenate([flip, r1], axis=0), 1)
    l2 = shift_z(jnp.concatenate([l1, flip], axis=0), -1)
    r3, l3 = shift_z(r2, 1), shift_z(l2, -1)
    half = TILE // 2
    r4, l4 = shift_z(r3[: TILE + half], 1), shift_z(l3[half:], -1)
    r5, l5 = shift_z(r4[:half], 1), shift_z(l4[TILE:], -1)
    return own, flip, r1, l1, r2, r3, l2, l3, r4, l4, r5, l5


def attend(nblk, here_ref, order_ref, list_ref, count_ref, *refs):
    blocks = refs[:nblk]
    w_ref, cot_ref, out_ref, sum_ref, kv_rows, kv_cols, q_cols, acc = refs[nblk:]
    scale = HEAD_DIM ** (-0.5)
    tiles = kv_rows.shape[0]
    w = w_ref[...]
    w = jnp.concatenate([w[HEAD_DIM:], w[:HEAD_DIM]], axis=0)
    slot = 0
    for blk in tiles_of(blocks):
        qkv = dot(blk, w, 1, 1).astype(BF)
        for r in range(blk.shape[0] // TILE):
            tile = order_ref[slot]
            slot += 1
            piece = qkv[r * TILE : (r + 1) * TILE]
            kv = piece[:, :TILE]
            kv_rows[tile] = kv
            kv_cols[tile] = kv.T
            q_cols[tile] = piece[:, TILE:].T
    acc[...] = jnp.zeros_like(acc)
    zero = jnp.zeros((HEAD_DIM, TILE), BF)

    def step(a, _):
        left = jnp.concatenate([q_cols[a], zero], axis=0)
        right = jnp.concatenate([zero, cot_ref[a, :HEAD_DIM, :]], axis=0)
        both = jnp.concatenate([left, right], axis=1)
        keys = [list_ref[a, t] for t in range(TOP)]
        count = count_ref[a]
        rows = jnp.concatenate([kv_rows[j] for j in keys], axis=0)
        prod = dot(rows, both, 1, 0)
        raw = prod[:, :TILE]
        dprobs = prod[:, TILE:]
        parts = [raw[t * TILE : (t + 1) * TILE] for t in range(TOP)]
        raw = jnp.concatenate(
            parts[:1] + [jnp.where(t < count, parts[t], -1e30) for t in range(1, TOP)], axis=0
        )
        top = jnp.max(raw, axis=0, keepdims=True)
        expo = jnp.exp((raw - top) * scale)
        probs = expo * (1.0 / jnp.sum(expo, axis=0, keepdims=True))
        delta = jnp.sum(probs * dprobs, axis=0, keepdims=True)
        dscores = (probs * ((dprobs - delta) * scale)).astype(BF)
        pair = jnp.concatenate([dscores, probs.astype(BF)], axis=1)
        cols = jnp.concatenate([kv_cols[j] for j in keys], axis=1)
        out = dot(cols, pair, 1, 0)
        out_ref[a, :HEAD_DIM, :] = out[:HEAD_DIM, :TILE].astype(BF)
        out_ref[a, 3 * HEAD_DIM :, :] = out[HEAD_DIM:, TILE:].astype(BF)
        both_t = jnp.concatenate([left.T, right.T], axis=0)
        back = dot(pair, both_t, 1, 0)
        for t in range(TOP):
            acc[keys[t]] += back[t * TILE : (t + 1) * TILE]
        return 0

    lax.fori_loop(0, tiles, step, 0, unroll=2)
    for a in range(tiles):
        out_ref[a, HEAD_DIM : 3 * HEAD_DIM, :] = acc[a].astype(BF).T

    total, slot = None, 0
    for blk in tiles_of(blocks):
        n = blk.shape[0] // TILE
        left = [out_ref[order_ref[slot + r], : 3 * HEAD_DIM, :] for r in range(n)]
        slot += n
        part = dot(jnp.concatenate(left, axis=1), blk, 1, 0)
        total = part if total is None else total + part
    rows = sum_ref.shape[1]
    here = here_ref[0]
    for i in range(DP):
        sum_ref[mirror(i) ^ here] = total[i * rows : (i + 1) * rows]


def attention(here, order, tile_list, counts, blocks, w_head, cot_t):
    tiles = tile_list.shape[0]
    rows, depth = w_head.shape[0] // DP, w_head.shape[1]
    return pl.pallas_call(
        functools.partial(attend, len(blocks)),
        out_shape=(
            jax.ShapeDtypeStruct((tiles, 4 * HEAD_DIM, TILE), BF),
            jax.ShapeDtypeStruct((DP, rows, depth), F32),
        ),
        in_specs=[SM, SM, SM, SM] + [VM] * (len(blocks) + 2),
        out_specs=(VM, VM),
        scratch_shapes=[
            pltpu.VMEM((tiles, TILE, 2 * HEAD_DIM), BF),
            pltpu.VMEM((tiles, 2 * HEAD_DIM, TILE), BF),
            pltpu.VMEM((tiles, HEAD_DIM, TILE), BF),
            pltpu.VMEM((tiles, TILE, 2 * HEAD_DIM), F32),
        ],
        compiler_params=PARAMS,
        name="attend",
    )(here, order, tile_list, counts, *blocks, w_head, cot_t)


def input_sum(both_ref, w_ref, att_ref, out_ref, sorted_ref):
    heads = both_ref.shape[0]
    att_ref[...] = jnp.concatenate(
        [both_ref[h, 3 * HEAD_DIM :, :] for h in range(heads)], axis=0
    ).T
    rows = 3 * HEAD_DIM // DP
    for h in range(heads):
        part = both_ref[h, : 3 * HEAD_DIM, :].astype(F32)
        for d in range(DP):
            at = (d * heads + h) * rows
            sorted_ref[at : at + rows, :] = part[d * rows : (d + 1) * rows]
    left = sorted_ref[...].astype(BF).T
    out_ref[...] = dot(left, w_ref[...], 1, 0).astype(BF)


def input_grad(both, w_all):
    heads = both.shape[0]
    return pl.pallas_call(
        input_sum,
        out_shape=(
            jax.ShapeDtypeStruct((TILE, heads * HEAD_DIM), BF),
            jax.ShapeDtypeStruct((TILE, w_all.shape[1]), BF),
        ),
        in_specs=[VM, VM],
        out_specs=(VM, VM),
        scratch_shapes=[pltpu.VMEM((w_all.shape[0], TILE), F32)],
        compiler_params=PARAMS,
        name="input_sum",
    )(both, w_all)


def shards(tokens, qkv_weight, key_tiles, key_counts, cotangent):
    heads = SEQ
    depth = tokens.shape[2]
    tiles = key_tiles.shape[1]
    dp, seq = lax.axis_index("dp"), lax.axis_index("seq")
    z, y_hi = seq // YH, seq % YH
    grad_scale = (DP * tiles * TILE) ** (-0.5)

    blocks = gather_scene(tokens[0])

    own_rows = qkv_weight[0]
    rows = own_rows.shape[0]
    lanes = rows * depth // TILE
    cot_t = cotangent[0].T.reshape(heads, HEAD_DIM, TILE)
    copies = jnp.broadcast_to(own_rows.reshape(lanes, TILE)[None], (heads, lanes, TILE))
    mixed = jnp.concatenate([cot_t, copies], axis=1)
    mixed = lax.all_to_all(mixed, "seq", 0, 0, tiled=True)
    w_seq = mixed[:, HEAD_DIM:].reshape(heads * rows, depth)
    w_seq, _ = lax.optimization_barrier((w_seq, (blocks[4], blocks[6])))
    w_all = lax.all_gather(w_seq, "dp", axis=0, tiled=True)

    own_rows, _ = lax.optimization_barrier((own_rows, mixed))
    w_head = spread(own_rows, "dp", DP).reshape(DP * rows, depth)

    here = mirror(dp)[None].astype(jnp.int32)
    order = tile_places(z, y_hi)
    both, sums = attention(here, order, key_tiles[0], key_counts[0], blocks, w_head, mixed)
    both = lax.all_to_all(both, "seq", 0, 0, tiled=True)

    for bit in (1, 2, 4, 8, 16):
        half = sums.shape[0] // 2
        sums = sums[:half] + swap_dp(sums[half:].astype(BF), bit).astype(F32)
        if bit == 1:
            w_all, sums = lax.optimization_barrier((w_all, sums))
    grad_weight = sums * grad_scale

    attended, grad_input = input_grad(both, w_all)
    return (attended[None], grad_input[None], grad_weight)


def solution(mesh):
    in_specs = (
        P("dp", "seq", None),
        P("seq", "dp", None),
        P("dp", None, None),
        P("dp", None),
        P("dp", "seq", None),
    )
    out_specs = (P("dp", "seq", None), P("dp", "seq", None), P("seq", "dp", None))
    return jax.shard_map(shards, mesh=mesh, in_specs=in_specs, out_specs=out_specs, check_vma=False)
```

```python
import functools

import jax
import jax.numpy as jnp
from jax import lax
from jax.experimental import pallas as pl
from jax.experimental.pallas import tpu as pltpu
from jax.sharding import PartitionSpec as P

HEAD_DIM = 64
TILE = 128
TOP = 4
BF = jnp.bfloat16
F32 = jnp.float32
VM = pl.BlockSpec(memory_space=pltpu.VMEM)
SM = pl.BlockSpec(memory_space=pltpu.SMEM)
PARAMS = pltpu.CompilerParams(vmem_limit_bytes=32 * 2**20)

YL, XN, CORES, ZN, YH = 4, 4, 2, 8, 2
DP = YL * XN * CORES
SEQ = ZN * YH


def dot(a, b, ca, cb):
    return lax.dot_general(a, b, (((ca,), (cb,)), ((), ())), preferred_element_type=F32)


def flip_y(x):
    return lax.ppermute(x, "seq", [(s, s ^ 1) for s in range(SEQ)])


def shift_z(x, k):
    return lax.ppermute(x, "seq", [(s, (s + YH * k) % SEQ) for s in range(SEQ)])


def swap_dp(x, bit):
    return lax.ppermute(x, "dp", [(d, d ^ bit) for d in range(DP)])


def spread(x, axis, n):
    copies = jnp.broadcast_to(x[None], (n, *x.shape))
    return lax.all_to_all(copies, axis, 0, 0, tiled=True)


def mirror(dp):
    return sum(((dp >> k) & 1) << (4 - k) for k in range(5))


def tiles_of(blocks):
    own, flip, r1, l1, r2, r3, l2, l3, r4, l4, far = blocks
    half = TILE // 2
    yield from (own[...], flip[...], r1[...], l1[...])
    for pair in (r2, r3, l2, l3):
        yield pair[...]
    yield r4[:TILE]
    yield l4[half:]
    yield jnp.concatenate([r4[TILE:], l4[:half]], axis=0)
    yield far[...]


def tile_places(z, y_hi):
    steps = [(0, 0), (0, 1), (-1, 0), (1, 0), (-1, 1), (-2, 0), (-2, 1), (-3, 0)]
    steps += [(2, 0), (1, 1), (3, 0), (2, 1), (-3, 1), (3, 1), (4, 0), (4, 1)]
    places = [lax.rem(z + k + ZN, ZN) * YH + lax.rem(y_hi + j, YH) for k, j in steps]
    return jnp.stack(places).astype(jnp.int32)


def gather_scene(own):
    flip, r1, l1 = flip_y(own), shift_z(own, 1), shift_z(own, -1)
    r2 = shift_z(jnp.concatenate([flip, r1], axis=0), 1)
    l2 = shift_z(jnp.concatenate([l1, flip], axis=0), -1)
    r3, l3 = shift_z(r2, 1), shift_z(l2, -1)
    half = TILE // 2
    r4, l4 = shift_z(r3[: TILE + half], 1), shift_z(l3[half:], -1)
    far = shift_z(flip, ZN // 2)
    return own, flip, r1, l1, r2, r3, l2, l3, r4, l4, far


def attend(nblk, here_ref, order_ref, list_ref, count_ref, *refs):
    blocks = refs[:nblk]
    w_ref, cot_ref, out_ref, sum_ref, kv_rows, kv_cols, q_cols, acc = refs[nblk:]
    scale = HEAD_DIM ** (-0.5)
    tiles = kv_rows.shape[0]
    w = w_ref[...]
    w = jnp.concatenate([w[HEAD_DIM:], w[:HEAD_DIM]], axis=0)
    slot = 0
    for blk in tiles_of(blocks):
        qkv = dot(blk, w, 1, 1).astype(BF)
        for r in range(blk.shape[0] // TILE):
            tile = order_ref[slot]
            slot += 1
            piece = qkv[r * TILE : (r + 1) * TILE]
            kv = piece[:, :TILE]
            kv_rows[tile] = kv
            kv_cols[tile] = kv.T
            q_cols[tile] = piece[:, TILE:].T
    acc[...] = jnp.zeros_like(acc)
    zero = jnp.zeros((HEAD_DIM, TILE), BF)

    def step(a, _):
        left = jnp.concatenate([q_cols[a], zero], axis=0)
        right = jnp.concatenate([zero, cot_ref[a, :HEAD_DIM, :]], axis=0)
        both = jnp.concatenate([left, right], axis=1)
        keys = [list_ref[a, t] for t in range(TOP)]
        count = count_ref[a]
        rows = jnp.concatenate([kv_rows[j] for j in keys], axis=0)
        prod = dot(rows, both, 1, 0)
        raw = prod[:, :TILE]
        dprobs = prod[:, TILE:]
        parts = [raw[t * TILE : (t + 1) * TILE] for t in range(TOP)]
        raw = jnp.concatenate(
            parts[:1] + [jnp.where(t < count, parts[t], -1e30) for t in range(1, TOP)], axis=0
        )
        top = jnp.max(raw, axis=0, keepdims=True)
        expo = jnp.exp((raw - top) * scale)
        probs = expo * (1.0 / jnp.sum(expo, axis=0, keepdims=True))
        delta = jnp.sum(probs * dprobs, axis=0, keepdims=True)
        dscores = (probs * ((dprobs - delta) * scale)).astype(BF)
        pair = jnp.concatenate([dscores, probs.astype(BF)], axis=1)
        cols = jnp.concatenate([kv_cols[j] for j in keys], axis=1)
        out = dot(cols, pair, 1, 0)
        out_ref[a, :HEAD_DIM, :] = out[:HEAD_DIM, :TILE].astype(BF)
        out_ref[a, 3 * HEAD_DIM :, :] = out[HEAD_DIM:, TILE:].astype(BF)
        both_t = jnp.concatenate([left.T, right.T], axis=0)
        back = dot(pair, both_t, 1, 0)
        for t in range(TOP):
            acc[keys[t]] += back[t * TILE : (t + 1) * TILE]
        return 0

    lax.fori_loop(0, tiles, step, 0, unroll=2)
    for a in range(tiles):
        out_ref[a, HEAD_DIM : 3 * HEAD_DIM, :] = acc[a].astype(BF).T

    total, slot = None, 0
    for blk in tiles_of(blocks):
        n = blk.shape[0] // TILE
        left = [out_ref[order_ref[slot + r], : 3 * HEAD_DIM, :] for r in range(n)]
        slot += n
        part = dot(jnp.concatenate(left, axis=1), blk, 1, 0)
        total = part if total is None else total + part
    rows = sum_ref.shape[1]
    here = here_ref[0]
    for i in range(DP):
        sum_ref[mirror(i) ^ here] = total[i * rows : (i + 1) * rows]


def attention(here, order, tile_list, counts, blocks, w_head, cot_t):
    tiles = tile_list.shape[0]
    rows, depth = w_head.shape[0] // DP, w_head.shape[1]
    return pl.pallas_call(
        functools.partial(attend, len(blocks)),
        out_shape=(
            jax.ShapeDtypeStruct((tiles, 4 * HEAD_DIM, TILE), BF),
            jax.ShapeDtypeStruct((DP, rows, depth), F32),
        ),
        in_specs=[SM, SM, SM, SM] + [VM] * (len(blocks) + 2),
        out_specs=(VM, VM),
        scratch_shapes=[
            pltpu.VMEM((tiles, TILE, 2 * HEAD_DIM), BF),
            pltpu.VMEM((tiles, 2 * HEAD_DIM, TILE), BF),
            pltpu.VMEM((tiles, HEAD_DIM, TILE), BF),
            pltpu.VMEM((tiles, TILE, 2 * HEAD_DIM), F32),
        ],
        compiler_params=PARAMS,
        name="attend",
    )(here, order, tile_list, counts, *blocks, w_head, cot_t)


def input_sum(both_ref, w_ref, att_ref, out_ref, sorted_ref):
    heads = both_ref.shape[0]
    att_ref[...] = jnp.concatenate(
        [both_ref[h, 3 * HEAD_DIM :, :] for h in range(heads)], axis=0
    ).T
    rows = 3 * HEAD_DIM // DP
    for h in range(heads):
        part = both_ref[h, : 3 * HEAD_DIM, :].astype(F32)
        for d in range(DP):
            at = (d * heads + h) * rows
            sorted_ref[at : at + rows, :] = part[d * rows : (d + 1) * rows]
    left = sorted_ref[...].astype(BF).T
    out_ref[...] = dot(left, w_ref[...], 1, 0).astype(BF)


def input_grad(both, w_all):
    heads = both.shape[0]
    return pl.pallas_call(
        input_sum,
        out_shape=(
            jax.ShapeDtypeStruct((TILE, heads * HEAD_DIM), BF),
            jax.ShapeDtypeStruct((TILE, w_all.shape[1]), BF),
        ),
        in_specs=[VM, VM],
        out_specs=(VM, VM),
        scratch_shapes=[pltpu.VMEM((w_all.shape[0], TILE), F32)],
        compiler_params=PARAMS,
        name="input_sum",
    )(both, w_all)


def shards(tokens, qkv_weight, key_tiles, key_counts, cotangent):
    heads = SEQ
    depth = tokens.shape[2]
    tiles = key_tiles.shape[1]
    dp, seq = lax.axis_index("dp"), lax.axis_index("seq")
    z, y_hi = seq // YH, seq % YH
    grad_scale = (DP * tiles * TILE) ** (-0.5)

    blocks = gather_scene(tokens[0])

    own_rows = qkv_weight[0]
    rows = own_rows.shape[0]
    lanes = rows * depth // TILE
    cot_t = cotangent[0].T.reshape(heads, HEAD_DIM, TILE)
    copies = jnp.broadcast_to(own_rows.reshape(lanes, TILE)[None], (heads, lanes, TILE))
    mixed = jnp.concatenate([cot_t, copies], axis=1)
    mixed = lax.all_to_all(mixed, "seq", 0, 0, tiled=True)
    w_seq = mixed[:, HEAD_DIM:].reshape(heads * rows, depth)
    w_seq, _ = lax.optimization_barrier((w_seq, (blocks[4], blocks[6])))
    w_all = lax.all_gather(w_seq, "dp", axis=0, tiled=True)

    own_rows, _ = lax.optimization_barrier((own_rows, mixed))
    w_head = spread(own_rows, "dp", DP).reshape(DP * rows, depth)

    here = mirror(dp)[None].astype(jnp.int32)
    order = tile_places(z, y_hi)
    both, sums = attention(here, order, key_tiles[0], key_counts[0], blocks, w_head, mixed)
    both = lax.all_to_all(both, "seq", 0, 0, tiled=True)

    for bit in (1, 2, 4, 8, 16):
        half = sums.shape[0] // 2
        sums = sums[:half] + swap_dp(sums[half:].astype(BF), bit).astype(F32)
        if bit == 1:
            w_all, sums = lax.optimization_barrier((w_all, sums))
    grad_weight = sums * grad_scale

    attended, grad_input = input_grad(both, w_all)
    return (attended[None], grad_input[None], grad_weight)


def solution(mesh):
    in_specs = (
        P("dp", "seq", None),
        P("seq", "dp", None),
        P("dp", None, None),
        P("dp", None),
        P("dp", "seq", None),
    )
    out_specs = (P("dp", "seq", None), P("dp", "seq", None), P("seq", "dp", None))
    return jax.shard_map(shards, mesh=mesh, in_specs=in_specs, out_specs=out_specs, check_vma=False)
```

```python
import functools

import jax
import jax.numpy as jnp
from jax import lax
from jax.experimental import pallas as pl
from jax.experimental.pallas import tpu as pltpu
from jax.sharding import PartitionSpec as P

HEAD_DIM = 64
TILE = 128
TOP = 4
BF = jnp.bfloat16
F32 = jnp.float32
VM = pl.BlockSpec(memory_space=pltpu.VMEM)
SM = pl.BlockSpec(memory_space=pltpu.SMEM)
HBM = pl.BlockSpec(memory_space=pltpu.HBM)
PARAMS = pltpu.CompilerParams(vmem_limit_bytes=32 * 2**20)

YL, XN, CORES, ZN, YH = 4, 4, 2, 8, 2
DP = YL * XN * CORES
SEQ = ZN * YH


def dot(a, b, ca, cb):
    return lax.dot_general(a, b, (((ca,), (cb,)), ((), ())), preferred_element_type=F32)


def flip_y(x):
    return lax.ppermute(x, "seq", [(s, s ^ 1) for s in range(SEQ)])


def shift_z(x, k):
    return lax.ppermute(x, "seq", [(s, (s + YH * k) % SEQ) for s in range(SEQ)])


def swap_dp(x, bit):
    return lax.ppermute(x, "dp", [(d, d ^ bit) for d in range(DP)])


def spread(x, axis, n):
    copies = jnp.broadcast_to(x[None], (n, *x.shape))
    return lax.all_to_all(copies, axis, 0, 0, tiled=True)


def mirror(dp):
    return sum(((dp >> k) & 1) << (4 - k) for k in range(5))


def tiles_of(blocks):
    own, flip, r1, l1, r2, r3, l2, l3, r4, l4, far = blocks
    half = TILE // 2
    yield from (own[...], flip[...], r1[...], l1[...])
    for pair in (r2, r3, l2, l3):
        yield pair[...]
    yield r4[:TILE]
    yield l4[half:]
    yield jnp.concatenate([r4[TILE:], l4[:half]], axis=0)
    yield far[...]


def tile_places(z, y_hi):
    steps = [(0, 0), (0, 1), (-1, 0), (1, 0), (-1, 1), (-2, 0), (-2, 1), (-3, 0)]
    steps += [(2, 0), (1, 1), (3, 0), (2, 1), (-3, 1), (3, 1), (4, 0), (4, 1)]
    places = [lax.rem(z + k + ZN, ZN) * YH + lax.rem(y_hi + j, YH) for k, j in steps]
    return jnp.stack(places).astype(jnp.int32)


def gather_scene(own):
    flip, r1, l1 = flip_y(own), shift_z(own, 1), shift_z(own, -1)
    r2 = shift_z(jnp.concatenate([flip, r1], axis=0), 1)
    l2 = shift_z(jnp.concatenate([l1, flip], axis=0), -1)
    r3, l3 = shift_z(r2, 1), shift_z(l2, -1)
    half = TILE // 2
    r4, l4 = shift_z(r3[: TILE + half], 1), shift_z(l3[half:], -1)
    far = shift_z(flip, ZN // 2)
    return own, flip, r1, l1, r2, r3, l2, l3, r4, l4, far


def attend(nblk, here_ref, order_ref, list_ref, count_ref, *refs):
    blocks = refs[:nblk]
    w_ref, cot_ref, out_ref, keep_ref, send_ref, kv_rows, kv_cols, q_cols, acc = refs[nblk:]
    scale = HEAD_DIM ** (-0.5)
    tiles = kv_rows.shape[0]
    w = w_ref[...]
    w = jnp.concatenate([w[HEAD_DIM:], w[:HEAD_DIM]], axis=0)
    slot = 0
    for blk in tiles_of(blocks):
        qkv = dot(blk, w, 1, 1).astype(BF)
        for r in range(blk.shape[0] // TILE):
            tile = order_ref[slot]
            slot += 1
            piece = qkv[r * TILE : (r + 1) * TILE]
            kv = piece[:, :TILE]
            kv_rows[tile] = kv
            kv_cols[tile] = kv.T
            q_cols[tile] = piece[:, TILE:].T
    acc[...] = jnp.zeros_like(acc)
    zero = jnp.zeros((HEAD_DIM, TILE), BF)

    def step(a, _):
        left = jnp.concatenate([q_cols[a], zero], axis=0)
        right = jnp.concatenate([zero, cot_ref[a, :HEAD_DIM, :]], axis=0)
        both = jnp.concatenate([left, right], axis=1)
        keys = [list_ref[a, t] for t in range(TOP)]
        count = count_ref[a]
        rows = jnp.concatenate([kv_rows[j] for j in keys], axis=0)
        prod = dot(rows, both, 1, 0)
        raw = prod[:, :TILE]
        dprobs = prod[:, TILE:]
        parts = [raw[t * TILE : (t + 1) * TILE] for t in range(TOP)]
        raw = jnp.concatenate(
            parts[:1] + [jnp.where(t < count, parts[t], -1e30) for t in range(1, TOP)], axis=0
        )
        top = jnp.max(raw, axis=0, keepdims=True)
        expo = jnp.exp((raw - top) * scale)
        probs = expo * (1.0 / jnp.sum(expo, axis=0, keepdims=True))
        delta = jnp.sum(probs * dprobs, axis=0, keepdims=True)
        dscores = (probs * ((dprobs - delta) * scale)).astype(BF)
        pair = jnp.concatenate([dscores, probs.astype(BF)], axis=1)
        cols = jnp.concatenate([kv_cols[j] for j in keys], axis=1)
        out = dot(cols, pair, 1, 0)
        out_ref[a, :HEAD_DIM, :] = out[:HEAD_DIM, :TILE].astype(BF)
        out_ref[a, 3 * HEAD_DIM :, :] = out[HEAD_DIM:, TILE:].astype(BF)
        both_t = jnp.concatenate([left.T, right.T], axis=0)
        back = dot(pair, both_t, 1, 0)
        for t in range(TOP):
            acc[keys[t]] += back[t * TILE : (t + 1) * TILE]
        return 0

    lax.fori_loop(0, tiles, step, 0, unroll=2)
    for a in range(tiles):
        out_ref[a, HEAD_DIM : 3 * HEAD_DIM, :] = acc[a].astype(BF).T

    total, slot = None, 0
    for blk in tiles_of(blocks):
        n = blk.shape[0] // TILE
        left = [out_ref[order_ref[slot + r], : 3 * HEAD_DIM, :] for r in range(n)]
        slot += n
        part = dot(jnp.concatenate(left, axis=1), blk, 1, 0)
        total = part if total is None else total + part
    rows = keep_ref.shape[1]
    here = here_ref[0]
    first = here < DP // 2
    for i in range(0, DP, CORES):
        even, odd = total[i * rows : (i + 1) * rows], total[(i + 1) * rows : (i + 2) * rows]
        at = (mirror(i) ^ here) % (DP // 2)
        keep_ref[at] = jnp.where(first, even, odd)
        send_ref[at] = jnp.where(first, odd, even).astype(BF)


def attention(here, order, tile_list, counts, blocks, w_head, cot_t):
    tiles = tile_list.shape[0]
    rows, depth = w_head.shape[0] // DP, w_head.shape[1]
    outs = (
        ((tiles, 4 * HEAD_DIM, TILE), BF),
        ((DP // CORES, rows, depth), F32),
        ((DP // CORES, rows, depth), BF),
    )
    return pl.pallas_call(
        functools.partial(attend, len(blocks)),
        out_shape=tuple(jax.ShapeDtypeStruct(*o) for o in outs),
        out_specs=(VM,) * 3,
        in_specs=[SM, SM, SM, SM] + [VM] * (len(blocks) + 2),
        scratch_shapes=[
            pltpu.VMEM((tiles, TILE, 2 * HEAD_DIM), BF),
            pltpu.VMEM((tiles, 2 * HEAD_DIM, TILE), BF),
            pltpu.VMEM((tiles, HEAD_DIM, TILE), BF),
            pltpu.VMEM((tiles, TILE, 2 * HEAD_DIM), F32),
        ],
        compiler_params=PARAMS,
        name="attend",
    )(here, order, tile_list, counts, *blocks, w_head, cot_t)


def input_sum(both_ref, w_ref, att_ref, out_ref, w_here, sorted_ref, sems):
    heads = both_ref.shape[0]
    parts = sems.shape[0]
    deep = w_here.shape[0] // parts
    copies = []
    for p in range(parts):
        span = pl.ds(p * deep, deep)
        copies.append(pltpu.make_async_copy(w_ref.at[span], w_here.at[span], sems.at[p]))
        copies[-1].start()
    att_ref[...] = jnp.concatenate(
        [both_ref[h, 3 * HEAD_DIM :, :] for h in range(heads)], axis=0
    ).T
    rows = 3 * HEAD_DIM // DP
    for h in range(heads):
        part = both_ref[h, : 3 * HEAD_DIM, :].astype(F32)
        for d in range(DP):
            at = (d * heads + h) * rows
            sorted_ref[at : at + rows, :] = part[d * rows : (d + 1) * rows]
    total = None
    for p in range(parts):
        left = sorted_ref[p * deep : (p + 1) * deep, :].astype(BF).T
        copies[p].wait()
        part = dot(left, w_here[p * deep : (p + 1) * deep, :], 1, 0)
        total = part if total is None else total + part
    out_ref[...] = total.astype(BF)


def input_grad(both, w_all):
    heads = both.shape[0]
    deep, depth = w_all.shape
    return pl.pallas_call(
        input_sum,
        out_shape=(
            jax.ShapeDtypeStruct((TILE, heads * HEAD_DIM), BF),
            jax.ShapeDtypeStruct((TILE, depth), BF),
        ),
        in_specs=[VM, HBM],
        out_specs=(VM, VM),
        scratch_shapes=[
            pltpu.VMEM((deep, depth), BF),
            pltpu.VMEM((deep, TILE), F32),
            pltpu.SemaphoreType.DMA((4,)),
        ],
        compiler_params=pltpu.CompilerParams(vmem_limit_bytes=58 * 2**20),
        name="input_sum",
    )(both, w_all)


def shards(tokens, qkv_weight, key_tiles, key_counts, cotangent):
    heads = SEQ
    depth = tokens.shape[2]
    tiles = key_tiles.shape[1]
    dp, seq = lax.axis_index("dp"), lax.axis_index("seq")
    z, y_hi = seq // YH, seq % YH
    grad_scale = (DP * tiles * TILE) ** (-0.5)

    blocks = gather_scene(tokens[0])

    own_rows = qkv_weight[0]
    rows = own_rows.shape[0]
    lanes = rows * depth // TILE
    cot_t = cotangent[0].T.reshape(heads, HEAD_DIM, TILE)
    copies = jnp.broadcast_to(own_rows.reshape(lanes, TILE)[None], (heads, lanes, TILE))
    mixed = jnp.concatenate([cot_t, copies], axis=1)
    mixed = lax.all_to_all(mixed, "seq", 0, 0, tiled=True)
    w_seq = mixed[:, HEAD_DIM:].reshape(heads * rows, depth)
    w_seq, _ = lax.optimization_barrier((w_seq, (blocks[4], blocks[6])))
    w_all = lax.all_gather(w_seq, "dp", axis=0, tiled=True)

    own_rows, _ = lax.optimization_barrier((own_rows, mixed))
    w_head = spread(own_rows, "dp", DP).reshape(DP * rows, depth)

    here = mirror(dp)[None].astype(jnp.int32)
    order = tile_places(z, y_hi)
    both, keep, send = attention(here, order, key_tiles[0], key_counts[0], blocks, w_head, mixed)
    both = lax.all_to_all(both, "seq", 0, 0, tiled=True)

    sums = keep + swap_dp(send, 1).astype(F32)
    for bit in (2, 4, 8, 16):
        if bit == 8:
            sums, both = lax.optimization_barrier((sums, both))
        half = sums.shape[0] // 2
        sums = sums[:half] + swap_dp(sums[half:].astype(BF), bit).astype(F32)
        if bit == 8:
            attended, grad_input = input_grad(both, w_all)
            sums, attended = lax.optimization_barrier((sums, attended))
    grad_weight = sums * grad_scale

    return (attended[None], grad_input[None], grad_weight)


def solution(mesh):
    in_specs = (
        P("dp", "seq", None),
        P("seq", "dp", None),
        P("dp", None, None),
        P("dp", None),
        P("dp", "seq", None),
    )
    out_specs = (P("dp", "seq", None), P("dp", "seq", None), P("seq", "dp", None))
    return jax.shard_map(shards, mesh=mesh, in_specs=in_specs, out_specs=out_specs, check_vma=False)
```

```python
import functools

import jax
import jax.numpy as jnp
from jax import lax
from jax.experimental import pallas as pl
from jax.experimental.pallas import tpu as pltpu
from jax.sharding import PartitionSpec as P

HEAD_DIM = 64
TILE = 128
TOP = 4
BF = jnp.bfloat16
F32 = jnp.float32
VM = pl.BlockSpec(memory_space=pltpu.VMEM)
SM = pl.BlockSpec(memory_space=pltpu.SMEM)
PARAMS = pltpu.CompilerParams(vmem_limit_bytes=32 * 2**20)

YL, XN, CORES, ZN, YH = 4, 4, 2, 8, 2
DP = YL * XN * CORES
SEQ = ZN * YH


def dot(a, b, ca, cb):
    return lax.dot_general(a, b, (((ca,), (cb,)), ((), ())), preferred_element_type=F32)


def flip_y(x):
    return lax.ppermute(x, "seq", [(s, s ^ 1) for s in range(SEQ)])


def shift_z(x, k):
    return lax.ppermute(x, "seq", [(s, (s + YH * k) % SEQ) for s in range(SEQ)])


def swap_dp(x, bit):
    return lax.ppermute(x, "dp", [(d, d ^ bit) for d in range(DP)])


def spread(x, axis, n):
    copies = jnp.broadcast_to(x[None], (n, *x.shape))
    return lax.all_to_all(copies, axis, 0, 0, tiled=True)


def mirror(dp):
    return sum(((dp >> k) & 1) << (4 - k) for k in range(5))


def tiles_of(blocks):
    *whole, r3, l3, r4, l4 = blocks
    half = TILE // 2
    for block in whole:
        yield block[...]
    yield r3[:TILE]
    yield l3[half:]
    yield jnp.concatenate([r3[TILE:], l3[:half]], axis=0)
    yield jnp.concatenate([r4[...], l4[...]], axis=0)


def tile_places(z, y_hi):
    steps = [(0, 0), (0, 1), (-1, 0), (1, 0), (-2, 0), (2, 0), (-1, 1), (-3, 0), (3, 0), (1, 1)]
    steps += [(-2, 1), (2, 1), (-3, 1), (3, 1), (4, 0), (4, 1)]
    places = [lax.rem(z + k + ZN, ZN) * YH + lax.rem(y_hi + j, YH) for k, j in steps]
    return jnp.stack(places).astype(jnp.int32)


def gather_scene(own):
    half = TILE // 2
    flip = flip_y(own)
    r1, l1, r2, l2 = (shift_z(own, k) for k in (1, -1, 2, -2))
    flip, r1, l1 = lax.optimization_barrier((flip, r1, l1))
    right = shift_z(jnp.concatenate([flip, r2], axis=0), 1)
    left = shift_z(jnp.concatenate([l2, flip], axis=0), -1)
    ry, ly = shift_z(flip, 2), shift_z(flip, -2)
    r3 = shift_z(jnp.concatenate([ry, right[TILE : TILE + half]], axis=0), 1)
    l3 = shift_z(jnp.concatenate([left[half:TILE], ly], axis=0), -1)
    r4, l4 = shift_z(ry[:half], 2), shift_z(ly[half:], -2)
    return own, flip, r1, l1, r2, l2, right, left, ry, ly, r3, l3, r4, l4


def attend(nblk, here_ref, order_ref, list_ref, count_ref, *refs):
    blocks = refs[:nblk]
    w_ref, cot_ref, out_ref, keep_ref, send_ref, kv_rows, kv_cols, q_cols, acc = refs[nblk:]
    scale = HEAD_DIM ** (-0.5)
    tiles = kv_rows.shape[0]
    w = w_ref[...]
    w = jnp.concatenate([w[HEAD_DIM:], w[:HEAD_DIM]], axis=0)
    slot = 0
    for blk in tiles_of(blocks):
        qkv = dot(blk, w, 1, 1).astype(BF)
        for r in range(blk.shape[0] // TILE):
            tile = order_ref[slot]
            slot += 1
            piece = qkv[r * TILE : (r + 1) * TILE]
            kv = piece[:, :TILE]
            kv_rows[tile] = kv
            kv_cols[tile] = kv.T
            q_cols[tile] = piece[:, TILE:].T
    acc[...] = jnp.zeros_like(acc)
    zero = jnp.zeros((HEAD_DIM, TILE), BF)

    def step(a, _):
        left = jnp.concatenate([q_cols[a], zero], axis=0)
        right = jnp.concatenate([zero, cot_ref[a, :HEAD_DIM, :]], axis=0)
        both = jnp.concatenate([left, right], axis=1)
        keys = [list_ref[a, t] for t in range(TOP)]
        count = count_ref[a]
        rows = jnp.concatenate([kv_rows[j] for j in keys], axis=0)
        prod = dot(rows, both, 1, 0)
        raw = prod[:, :TILE]
        dprobs = prod[:, TILE:]
        parts = [raw[t * TILE : (t + 1) * TILE] for t in range(TOP)]
        raw = jnp.concatenate(
            parts[:1] + [jnp.where(t < count, parts[t], -1e30) for t in range(1, TOP)], axis=0
        )
        top = jnp.max(raw, axis=0, keepdims=True)
        expo = jnp.exp((raw - top) * scale)
        probs = expo * (1.0 / jnp.sum(expo, axis=0, keepdims=True))
        delta = jnp.sum(probs * dprobs, axis=0, keepdims=True)
        dscores = (probs * ((dprobs - delta) * scale)).astype(BF)
        pair = jnp.concatenate([dscores, probs.astype(BF)], axis=1)
        cols = jnp.concatenate([kv_cols[j] for j in keys], axis=1)
        out = dot(cols, pair, 1, 0)
        out_ref[a, :HEAD_DIM, :] = out[:HEAD_DIM, :TILE].astype(BF)
        out_ref[a, 3 * HEAD_DIM :, :] = out[HEAD_DIM:, TILE:].astype(BF)
        both_t = jnp.concatenate([left.T, right.T], axis=0)
        back = dot(pair, both_t, 1, 0)
        for t in range(TOP):
            acc[keys[t]] += back[t * TILE : (t + 1) * TILE]
        return 0

    lax.fori_loop(0, tiles, step, 0, unroll=2)
    for a in range(tiles):
        out_ref[a, HEAD_DIM : 3 * HEAD_DIM, :] = acc[a].astype(BF).T

    total, slot = None, 0
    for blk in tiles_of(blocks):
        n = blk.shape[0] // TILE
        left = [out_ref[order_ref[slot + r], : 3 * HEAD_DIM, :] for r in range(n)]
        slot += n
        part = dot(jnp.concatenate(left, axis=1), blk, 1, 0)
        total = part if total is None else total + part
    rows = keep_ref.shape[1]
    here = here_ref[0]
    first = here < DP // 2
    for i in range(0, DP, CORES):
        even, odd = total[i * rows : (i + 1) * rows], total[(i + 1) * rows : (i + 2) * rows]
        at = (mirror(i) ^ here) % (DP // 2)
        keep_ref[at] = jnp.where(first, even, odd)
        send_ref[at] = jnp.where(first, odd, even).astype(BF)


def attention(here, order, tile_list, counts, blocks, w_head, cot_t):
    tiles = tile_list.shape[0]
    rows, depth = w_head.shape[0] // DP, w_head.shape[1]
    outs = (
        ((tiles, 4 * HEAD_DIM, TILE), BF),
        ((DP // CORES, rows, depth), F32),
        ((DP // CORES, rows, depth), BF),
    )
    return pl.pallas_call(
        functools.partial(attend, len(blocks)),
        out_shape=tuple(jax.ShapeDtypeStruct(*o) for o in outs),
        out_specs=(VM,) * 3,
        in_specs=[SM, SM, SM, SM] + [VM] * (len(blocks) + 2),
        scratch_shapes=[
            pltpu.VMEM((tiles, TILE, 2 * HEAD_DIM), BF),
            pltpu.VMEM((tiles, 2 * HEAD_DIM, TILE), BF),
            pltpu.VMEM((tiles, HEAD_DIM, TILE), BF),
            pltpu.VMEM((tiles, TILE, 2 * HEAD_DIM), F32),
        ],
        compiler_params=PARAMS,
        name="attend",
    )(here, order, tile_list, counts, *blocks, w_head, cot_t)


def input_sum(both_ref, w_ref, att_ref, out_ref, sorted_ref):
    heads = both_ref.shape[0]
    att_ref[...] = jnp.concatenate(
        [both_ref[h, 3 * HEAD_DIM :, :] for h in range(heads)], axis=0
    ).T
    rows = 3 * HEAD_DIM // DP
    for h in range(heads):
        part = both_ref[h, : 3 * HEAD_DIM, :].astype(F32)
        for d in range(DP):
            at = (d * heads + h) * rows
            sorted_ref[at : at + rows, :] = part[d * rows : (d + 1) * rows]
    left = sorted_ref[...].astype(BF).T
    out_ref[...] = dot(left, w_ref[...], 1, 0).astype(BF)


def input_grad(both, w_all):
    heads = both.shape[0]
    return pl.pallas_call(
        input_sum,
        out_shape=(
            jax.ShapeDtypeStruct((TILE, heads * HEAD_DIM), BF),
            jax.ShapeDtypeStruct((TILE, w_all.shape[1]), BF),
        ),
        in_specs=[VM, VM],
        out_specs=(VM, VM),
        scratch_shapes=[pltpu.VMEM((w_all.shape[0], TILE), F32)],
        compiler_params=PARAMS,
        name="input_sum",
    )(both, w_all)


def shards(tokens, qkv_weight, key_tiles, key_counts, cotangent):
    heads = SEQ
    depth = tokens.shape[2]
    tiles = key_tiles.shape[1]
    dp, seq = lax.axis_index("dp"), lax.axis_index("seq")
    z, y_hi = seq // YH, seq % YH
    grad_scale = (DP * tiles * TILE) ** (-0.5)

    blocks = gather_scene(tokens[0])

    own_rows = qkv_weight[0]
    rows = own_rows.shape[0]
    lanes = rows * depth // TILE
    cot_t = cotangent[0].T.reshape(heads, HEAD_DIM, TILE)
    copies = jnp.broadcast_to(own_rows.reshape(lanes, TILE)[None], (heads, lanes, TILE))
    mixed = jnp.concatenate([cot_t, copies], axis=1)
    mixed = lax.all_to_all(mixed, "seq", 0, 0, tiled=True)
    w_seq = mixed[:, HEAD_DIM:].reshape(heads * rows, depth)
    w_seq, _ = lax.optimization_barrier((w_seq, blocks[6:10]))
    w_all = lax.all_gather(w_seq, "dp", axis=0, tiled=True)

    own_rows, _ = lax.optimization_barrier((own_rows, mixed))
    w_head = spread(own_rows, "dp", DP).reshape(DP * rows, depth)

    here = mirror(dp)[None].astype(jnp.int32)
    order = tile_places(z, y_hi)
    both, keep, send = attention(here, order, key_tiles[0], key_counts[0], blocks, w_head, mixed)
    both = lax.all_to_all(both, "seq", 0, 0, tiled=True)

    sums = keep + swap_dp(send, 1).astype(F32)
    w_all, sums = lax.optimization_barrier((w_all, sums))
    for bit in (2, 4, 8, 16):
        half = sums.shape[0] // 2
        sums = sums[:half] + swap_dp(sums[half:].astype(BF), bit).astype(F32)
    grad_weight = sums * grad_scale

    attended, grad_input = input_grad(both, w_all)
    return (attended[None], grad_input[None], grad_weight)


def solution(mesh):
    in_specs = (
        P("dp", "seq", None),
        P("seq", "dp", None),
        P("dp", None, None),
        P("dp", None),
        P("dp", "seq", None),
    )
    out_specs = (P("dp", "seq", None), P("dp", "seq", None), P("seq", "dp", None))
    return jax.shard_map(shards, mesh=mesh, in_specs=in_specs, out_specs=out_specs, check_vma=False)
```

```python
import functools

import jax
import jax.numpy as jnp
from jax import lax
from jax.experimental import pallas as pl
from jax.experimental.pallas import tpu as pltpu
from jax.sharding import PartitionSpec as P

HEAD_DIM = 64
TILE = 128
TOP = 4
BF = jnp.bfloat16
F32 = jnp.float32
VM = pl.BlockSpec(memory_space=pltpu.VMEM)
SM = pl.BlockSpec(memory_space=pltpu.SMEM)
PARAMS = pltpu.CompilerParams(vmem_limit_bytes=32 * 2**20)

YL, XN, CORES, ZN, YH = 4, 4, 2, 8, 2
DP = YL * XN * CORES
SEQ = ZN * YH


def dot(a, b, ca, cb):
    return lax.dot_general(a, b, (((ca,), (cb,)), ((), ())), preferred_element_type=F32)


def flip_y(x):
    return lax.ppermute(x, "seq", [(s, s ^ 1) for s in range(SEQ)])


def shift_z(x, k):
    return lax.ppermute(x, "seq", [(s, (s + YH * k) % SEQ) for s in range(SEQ)])


def swap_dp(x, bit):
    return lax.ppermute(x, "dp", [(d, d ^ bit) for d in range(DP)])


def spread(x, axis, n):
    copies = jnp.broadcast_to(x[None], (n, *x.shape))
    return lax.all_to_all(copies, axis, 0, 0, tiled=True)


def mirror(dp):
    return sum(((dp >> k) & 1) << (4 - k) for k in range(5))


def tiles_of(blocks):
    own, flip, r1, l1, r2, r3, l2, l3, r4, l4, far = blocks
    half = TILE // 2
    yield from (own[...], flip[...], r1[...], l1[...])
    for pair in (r2, r3, l2, l3):
        yield pair[...]
    yield r4[:TILE]
    yield l4[half:]
    yield jnp.concatenate([r4[TILE:], l4[:half]], axis=0)
    yield far[...]


def tile_places(z, y_hi):
    steps = [(0, 0), (0, 1), (-1, 0), (1, 0), (-1, 1), (-2, 0), (-2, 1), (-3, 0)]
    steps += [(2, 0), (1, 1), (3, 0), (2, 1), (-3, 1), (3, 1), (4, 0), (4, 1)]
    places = [lax.rem(z + k + ZN, ZN) * YH + lax.rem(y_hi + j, YH) for k, j in steps]
    return jnp.stack(places).astype(jnp.int32)


def gather_scene(own):
    flip, r1, l1 = flip_y(own), shift_z(own, 1), shift_z(own, -1)
    r2 = shift_z(jnp.concatenate([flip, r1], axis=0), 1)
    l2 = shift_z(jnp.concatenate([l1, flip], axis=0), -1)
    r3, l3 = shift_z(r2, 1), shift_z(l2, -1)
    half = TILE // 2
    r4, l4 = shift_z(r3[: TILE + half], 1), shift_z(l3[half:], -1)
    far = shift_z(flip, ZN // 2)
    return own, flip, r1, l1, r2, r3, l2, l3, r4, l4, far


def attend(nblk, here_ref, order_ref, list_ref, count_ref, *refs):
    blocks = refs[:nblk]
    w_ref, cot_ref, out_ref, keep_ref, send_ref, kv_rows, kv_cols, q_cols, acc = refs[nblk:]
    scale = HEAD_DIM ** (-0.5)
    tiles = kv_rows.shape[0]
    w = w_ref[...]
    w = jnp.concatenate([w[HEAD_DIM:], w[:HEAD_DIM]], axis=0)
    slot = 0
    for blk in tiles_of(blocks):
        qkv = dot(blk, w, 1, 1).astype(BF)
        for r in range(blk.shape[0] // TILE):
            tile = order_ref[slot]
            slot += 1
            piece = qkv[r * TILE : (r + 1) * TILE]
            kv = piece[:, :TILE]
            kv_rows[tile] = kv
            kv_cols[tile] = kv.T
            q_cols[tile] = piece[:, TILE:].T
    acc[...] = jnp.zeros_like(acc)
    zero = jnp.zeros((HEAD_DIM, TILE), BF)

    def step(a, _):
        left = jnp.concatenate([q_cols[a], zero], axis=0)
        right = jnp.concatenate([zero, cot_ref[a, :HEAD_DIM, :]], axis=0)
        both = jnp.concatenate([left, right], axis=1)
        keys = [list_ref[a, t] for t in range(TOP)]
        count = count_ref[a]
        rows = jnp.concatenate([kv_rows[j] for j in keys], axis=0)
        prod = dot(rows, both, 1, 0)
        raw = prod[:, :TILE]
        dprobs = prod[:, TILE:]
        parts = [raw[t * TILE : (t + 1) * TILE] for t in range(TOP)]
        raw = jnp.concatenate(
            parts[:1] + [jnp.where(t < count, parts[t], -1e30) for t in range(1, TOP)], axis=0
        )
        top = jnp.max(raw, axis=0, keepdims=True)
        expo = jnp.exp((raw - top) * scale)
        probs = expo * (1.0 / jnp.sum(expo, axis=0, keepdims=True))
        delta = jnp.sum(probs * dprobs, axis=0, keepdims=True)
        dscores = (probs * ((dprobs - delta) * scale)).astype(BF)
        pair = jnp.concatenate([dscores, probs.astype(BF)], axis=1)
        cols = jnp.concatenate([kv_cols[j] for j in keys], axis=1)
        out = dot(cols, pair, 1, 0)
        out_ref[a, :HEAD_DIM, :] = out[:HEAD_DIM, :TILE].astype(BF)
        out_ref[a, 3 * HEAD_DIM :, :] = out[HEAD_DIM:, TILE:].astype(BF)
        both_t = jnp.concatenate([left.T, right.T], axis=0)
        back = dot(pair, both_t, 1, 0)
        for t in range(TOP):
            acc[keys[t]] += back[t * TILE : (t + 1) * TILE]
        return 0

    lax.fori_loop(0, tiles, step, 0, unroll=2)
    for a in range(tiles):
        out_ref[a, HEAD_DIM : 3 * HEAD_DIM, :] = acc[a].astype(BF).T

    total, slot = None, 0
    for blk in tiles_of(blocks):
        n = blk.shape[0] // TILE
        left = [out_ref[order_ref[slot + r], : 3 * HEAD_DIM, :] for r in range(n)]
        slot += n
        part = dot(jnp.concatenate(left, axis=1), blk, 1, 0)
        total = part if total is None else total + part
    rows = keep_ref.shape[1]
    here = here_ref[0]
    first = here < DP // 2
    for i in range(0, DP, CORES):
        even, odd = total[i * rows : (i + 1) * rows], total[(i + 1) * rows : (i + 2) * rows]
        at = (mirror(i) ^ here) % (DP // 2)
        keep_ref[at] = jnp.where(first, even, odd)
        send_ref[at] = jnp.where(first, odd, even).astype(BF)


def attention(here, order, tile_list, counts, blocks, w_head, cot_t):
    tiles = tile_list.shape[0]
    rows, depth = w_head.shape[0] // DP, w_head.shape[1]
    outs = (
        ((tiles, 4 * HEAD_DIM, TILE), BF),
        ((DP // CORES, rows, depth), F32),
        ((DP // CORES, rows, depth), BF),
    )
    return pl.pallas_call(
        functools.partial(attend, len(blocks)),
        out_shape=tuple(jax.ShapeDtypeStruct(*o) for o in outs),
        out_specs=(VM,) * 3,
        in_specs=[SM, SM, SM, SM] + [VM] * (len(blocks) + 2),
        scratch_shapes=[
            pltpu.VMEM((tiles, TILE, 2 * HEAD_DIM), BF),
            pltpu.VMEM((tiles, 2 * HEAD_DIM, TILE), BF),
            pltpu.VMEM((tiles, HEAD_DIM, TILE), BF),
            pltpu.VMEM((tiles, TILE, 2 * HEAD_DIM), F32),
        ],
        compiler_params=PARAMS,
        name="attend",
    )(here, order, tile_list, counts, *blocks, w_head, cot_t)


def input_sum(both_ref, w_ref, att_ref, out_ref, sorted_ref):
    heads = both_ref.shape[0]
    att_ref[...] = jnp.concatenate(
        [both_ref[h, 3 * HEAD_DIM :, :] for h in range(heads)], axis=0
    ).T
    rows = 3 * HEAD_DIM // DP
    for h in range(heads):
        part = both_ref[h, : 3 * HEAD_DIM, :].astype(F32)
        for d in range(DP):
            at = (d * heads + h) * rows
            sorted_ref[at : at + rows, :] = part[d * rows : (d + 1) * rows]
    left = sorted_ref[...].astype(BF).T
    out_ref[...] = dot(left, w_ref[...], 1, 0).astype(BF)


def input_grad(both, w_all):
    heads = both.shape[0]
    return pl.pallas_call(
        input_sum,
        out_shape=(
            jax.ShapeDtypeStruct((TILE, heads * HEAD_DIM), BF),
            jax.ShapeDtypeStruct((TILE, w_all.shape[1]), BF),
        ),
        in_specs=[VM, VM],
        out_specs=(VM, VM),
        scratch_shapes=[pltpu.VMEM((w_all.shape[0], TILE), F32)],
        compiler_params=PARAMS,
        name="input_sum",
    )(both, w_all)


def shards(tokens, qkv_weight, key_tiles, key_counts, cotangent):
    heads = SEQ
    depth = tokens.shape[2]
    tiles = key_tiles.shape[1]
    dp, seq = lax.axis_index("dp"), lax.axis_index("seq")
    z, y_hi = seq // YH, seq % YH
    grad_scale = (DP * tiles * TILE) ** (-0.5)

    blocks = gather_scene(tokens[0])

    own_rows = qkv_weight[0]
    rows = own_rows.shape[0]
    lanes = rows * depth // TILE
    cot_t = cotangent[0].T.reshape(heads, HEAD_DIM, TILE)
    copies = jnp.broadcast_to(own_rows.reshape(lanes, TILE)[None], (heads, lanes, TILE))
    mixed = jnp.concatenate([cot_t, copies], axis=1)
    mixed = lax.all_to_all(mixed, "seq", 0, 0, tiled=True)
    w_seq = mixed[:, HEAD_DIM:].reshape(heads * rows, depth)
    w_seq, _ = lax.optimization_barrier((w_seq, (blocks[4], blocks[6])))
    w_all = lax.all_gather(w_seq, "dp", axis=0, tiled=True)

    own_rows, _ = lax.optimization_barrier((own_rows, mixed))
    w_head = spread(own_rows, "dp", DP).reshape(DP * rows, depth)

    here = mirror(dp)[None].astype(jnp.int32)
    order = tile_places(z, y_hi)
    both, keep, send = attention(here, order, key_tiles[0], key_counts[0], blocks, w_head, mixed)
    both = lax.all_to_all(both, "seq", 0, 0, tiled=True)

    sums = keep + swap_dp(send, 1).astype(F32)
    for bit in (2, 4, 8, 16):
        half = sums.shape[0] // 2
        sums = sums[:half] + swap_dp(sums[half:].astype(BF), bit).astype(F32)
    grad_weight = sums * grad_scale

    attended, grad_input = input_grad(both, w_all)
    return (attended[None], grad_input[None], grad_weight)


def solution(mesh):
    in_specs = (
        P("dp", "seq", None),
        P("seq", "dp", None),
        P("dp", None, None),
        P("dp", None),
        P("dp", "seq", None),
    )
    out_specs = (P("dp", "seq", None), P("dp", "seq", None), P("seq", "dp", None))
    return jax.shard_map(shards, mesh=mesh, in_specs=in_specs, out_specs=out_specs, check_vma=False)
```

```python
import functools

import jax
import jax.numpy as jnp
from jax import lax
from jax.experimental import pallas as pl
from jax.experimental.pallas import tpu as pltpu
from jax.sharding import PartitionSpec as P

HEAD_DIM = 64
TILE = 128
TOP = 4
BF = jnp.bfloat16
F32 = jnp.float32
VM = pl.BlockSpec(memory_space=pltpu.VMEM)
SM = pl.BlockSpec(memory_space=pltpu.SMEM)
PARAMS = pltpu.CompilerParams(vmem_limit_bytes=32 * 2**20)

YL, XN, CORES, ZN, YH = 4, 4, 2, 8, 2
DP = YL * XN * CORES
SEQ = ZN * YH


def dot(a, b, ca, cb):
    return lax.dot_general(a, b, (((ca,), (cb,)), ((), ())), preferred_element_type=F32)


def flip_y(x):
    return lax.ppermute(x, "seq", [(s, s ^ 1) for s in range(SEQ)])


def shift_z(x, k):
    return lax.ppermute(x, "seq", [(s, (s + YH * k) % SEQ) for s in range(SEQ)])


def swap_dp(x, bit):
    return lax.ppermute(x, "dp", [(d, d ^ bit) for d in range(DP)])


def spread(x, axis, n):
    copies = jnp.broadcast_to(x[None], (n, *x.shape))
    return lax.all_to_all(copies, axis, 0, 0, tiled=True)


def mirror(dp):
    return sum(((dp >> k) & 1) << (4 - k) for k in range(5))


def tiles_of(blocks):
    own, flip, r1, l1, r2, r3, l2, l3, r4, l4, far = blocks
    half = TILE // 2
    yield from (own[...], flip[...], r1[...], l1[...])
    for pair in (r2, r3, l2, l3):
        yield pair[...]
    yield r4[:TILE]
    yield l4[half:]
    yield jnp.concatenate([r4[TILE:], l4[:half]], axis=0)
    yield far[...]


def tile_places(z, y_hi):
    steps = [(0, 0), (0, 1), (-1, 0), (1, 0), (-1, 1), (-2, 0), (-2, 1), (-3, 0)]
    steps += [(2, 0), (1, 1), (3, 0), (2, 1), (-3, 1), (3, 1), (4, 0), (4, 1)]
    places = [lax.rem(z + k + ZN, ZN) * YH + lax.rem(y_hi + j, YH) for k, j in steps]
    return jnp.stack(places).astype(jnp.int32)


def gather_scene(own):
    flip, r1, l1 = flip_y(own), shift_z(own, 1), shift_z(own, -1)
    r2 = shift_z(jnp.concatenate([flip, r1], axis=0), 1)
    l2 = shift_z(jnp.concatenate([l1, flip], axis=0), -1)
    r3, l3 = shift_z(r2, 1), shift_z(l2, -1)
    half = TILE // 2
    r4, l4 = shift_z(r3[: TILE + half], 1), shift_z(l3[half:], -1)
    far = shift_z(flip, ZN // 2)
    return own, flip, r1, l1, r2, r3, l2, l3, r4, l4, far


def attend(nblk, here_ref, order_ref, list_ref, count_ref, *refs):
    blocks = refs[:nblk]
    w_ref, cot_ref, out_ref, keep_ref, send_ref, kv_rows, kv_cols, q_cols, acc = refs[nblk:]
    scale = HEAD_DIM ** (-0.5)
    tiles = kv_rows.shape[0]
    w = w_ref[...]
    w = jnp.concatenate([w[HEAD_DIM:], w[:HEAD_DIM]], axis=0)
    slot = 0
    for blk in tiles_of(blocks):
        qkv = dot(blk, w, 1, 1).astype(BF)
        for r in range(blk.shape[0] // TILE):
            tile = order_ref[slot]
            slot += 1
            piece = qkv[r * TILE : (r + 1) * TILE]
            kv = piece[:, :TILE]
            kv_rows[tile] = kv
            kv_cols[tile] = kv.T
            q_cols[tile] = piece[:, TILE:].T
    acc[...] = jnp.zeros_like(acc)
    zero = jnp.zeros((HEAD_DIM, TILE), BF)

    def step(a, _):
        left = jnp.concatenate([q_cols[a], zero], axis=0)
        right = jnp.concatenate([zero, cot_ref[a, :HEAD_DIM, :]], axis=0)
        both = jnp.concatenate([left, right], axis=1)
        keys = [list_ref[a, t] for t in range(TOP)]
        count = count_ref[a]
        rows = jnp.concatenate([kv_rows[j] for j in keys], axis=0)
        prod = dot(rows, both, 1, 0)
        raw = prod[:, :TILE]
        dprobs = prod[:, TILE:]
        parts = [raw[t * TILE : (t + 1) * TILE] for t in range(TOP)]
        raw = jnp.concatenate(
            parts[:1] + [jnp.where(t < count, parts[t], -1e30) for t in range(1, TOP)], axis=0
        )
        top = jnp.max(raw, axis=0, keepdims=True)
        expo = jnp.exp((raw - top) * scale)
        probs = expo * (1.0 / jnp.sum(expo, axis=0, keepdims=True))
        delta = jnp.sum(probs * dprobs, axis=0, keepdims=True)
        dscores = (probs * ((dprobs - delta) * scale)).astype(BF)
        pair = jnp.concatenate([dscores, probs.astype(BF)], axis=1)
        cols = jnp.concatenate([kv_cols[j] for j in keys], axis=1)
        out = dot(cols, pair, 1, 0)
        out_ref[a, :HEAD_DIM, :] = out[:HEAD_DIM, :TILE].astype(BF)
        out_ref[a, 3 * HEAD_DIM :, :] = out[HEAD_DIM:, TILE:].astype(BF)
        both_t = jnp.concatenate([left.T, right.T], axis=0)
        back = dot(pair, both_t, 1, 0)
        for t in range(TOP):
            acc[keys[t]] += back[t * TILE : (t + 1) * TILE]
        return 0

    lax.fori_loop(0, tiles, step, 0, unroll=2)
    for a in range(tiles):
        out_ref[a, HEAD_DIM : 3 * HEAD_DIM, :] = acc[a].astype(BF).T

    total, slot = None, 0
    for blk in tiles_of(blocks):
        n = blk.shape[0] // TILE
        left = [out_ref[order_ref[slot + r], : 3 * HEAD_DIM, :] for r in range(n)]
        slot += n
        part = dot(jnp.concatenate(left, axis=1), blk, 1, 0)
        total = part if total is None else total + part
    rows = keep_ref.shape[1]
    here = here_ref[0]
    first = here < DP // 2
    for i in range(0, DP, CORES):
        even, odd = total[i * rows : (i + 1) * rows], total[(i + 1) * rows : (i + 2) * rows]
        at = (mirror(i) ^ here) % (DP // 2)
        keep_ref[at] = jnp.where(first, even, odd)
        send_ref[at] = jnp.where(first, odd, even).astype(BF)


def attention(here, order, tile_list, counts, blocks, w_head, cot_t):
    tiles = tile_list.shape[0]
    rows, depth = w_head.shape[0] // DP, w_head.shape[1]
    outs = (
        ((tiles, 4 * HEAD_DIM, TILE), BF),
        ((DP // CORES, rows, depth), F32),
        ((DP // CORES, rows, depth), BF),
    )
    return pl.pallas_call(
        functools.partial(attend, len(blocks)),
        out_shape=tuple(jax.ShapeDtypeStruct(*o) for o in outs),
        out_specs=(VM,) * 3,
        in_specs=[SM, SM, SM, SM] + [VM] * (len(blocks) + 2),
        scratch_shapes=[
            pltpu.VMEM((tiles, TILE, 2 * HEAD_DIM), BF),
            pltpu.VMEM((tiles, 2 * HEAD_DIM, TILE), BF),
            pltpu.VMEM((tiles, HEAD_DIM, TILE), BF),
            pltpu.VMEM((tiles, TILE, 2 * HEAD_DIM), F32),
        ],
        compiler_params=PARAMS,
        name="attend",
    )(here, order, tile_list, counts, *blocks, w_head, cot_t)


def input_sum(both_ref, w_ref, att_ref, out_ref, sorted_ref):
    heads = both_ref.shape[0]
    att_ref[...] = jnp.concatenate(
        [both_ref[h, 3 * HEAD_DIM :, :] for h in range(heads)], axis=0
    ).T
    rows = 3 * HEAD_DIM // DP
    for h in range(heads):
        part = both_ref[h, : 3 * HEAD_DIM, :].astype(F32)
        for d in range(DP):
            at = (d * heads + h) * rows
            sorted_ref[at : at + rows, :] = part[d * rows : (d + 1) * rows]
    left = sorted_ref[...].astype(BF).T
    out_ref[...] = dot(left, w_ref[...], 1, 0).astype(BF)


def input_grad(both, w_all):
    heads = both.shape[0]
    return pl.pallas_call(
        input_sum,
        out_shape=(
            jax.ShapeDtypeStruct((TILE, heads * HEAD_DIM), BF),
            jax.ShapeDtypeStruct((TILE, w_all.shape[1]), BF),
        ),
        in_specs=[VM, VM],
        out_specs=(VM, VM),
        scratch_shapes=[pltpu.VMEM((w_all.shape[0], TILE), F32)],
        compiler_params=PARAMS,
        name="input_sum",
    )(both, w_all)


def shards(tokens, qkv_weight, key_tiles, key_counts, cotangent):
    heads = SEQ
    depth = tokens.shape[2]
    tiles = key_tiles.shape[1]
    dp, seq = lax.axis_index("dp"), lax.axis_index("seq")
    z, y_hi = seq // YH, seq % YH
    grad_scale = (DP * tiles * TILE) ** (-0.5)

    blocks = gather_scene(tokens[0])

    own_rows = qkv_weight[0]
    rows = own_rows.shape[0]
    lanes = rows * depth // TILE
    cot_t = cotangent[0].T.reshape(heads, HEAD_DIM, TILE)
    copies = jnp.broadcast_to(own_rows.reshape(lanes, TILE)[None], (heads, lanes, TILE))
    mixed = jnp.concatenate([cot_t, copies], axis=1)
    mixed = lax.all_to_all(mixed, "seq", 0, 0, tiled=True)
    w_seq = mixed[:, HEAD_DIM:].reshape(heads * rows, depth)
    w_seq, _ = lax.optimization_barrier((w_seq, (blocks[4], blocks[6])))
    w_all = lax.all_gather(w_seq, "dp", axis=0, tiled=True)

    own_rows, _ = lax.optimization_barrier((own_rows, mixed))
    w_head = spread(own_rows, "dp", DP).reshape(DP * rows, depth)

    here = mirror(dp)[None].astype(jnp.int32)
    order = tile_places(z, y_hi)
    both, keep, send = attention(here, order, key_tiles[0], key_counts[0], blocks, w_head, mixed)
    both = lax.all_to_all(both, "seq", 0, 0, tiled=True)

    came = swap_dp(send, 1)
    for bit in (2, 4, 8, 16):
        half = keep.shape[0] // 2
        send = (keep[half:] + came[half:].astype(F32)).astype(BF)
        keep = keep[:half] + came[:half].astype(F32)
        came = swap_dp(send, bit)
    grad_weight = (keep + came.astype(F32)) * grad_scale

    attended, grad_input = input_grad(both, w_all)
    return (attended[None], grad_input[None], grad_weight)


def solution(mesh):
    in_specs = (
        P("dp", "seq", None),
        P("seq", "dp", None),
        P("dp", None, None),
        P("dp", None),
        P("dp", "seq", None),
    )
    out_specs = (P("dp", "seq", None), P("dp", "seq", None), P("seq", "dp", None))
    return jax.shard_map(shards, mesh=mesh, in_specs=in_specs, out_specs=out_specs, check_vma=False)
```

```python
import functools

import jax
import jax.numpy as jnp
from jax import lax
from jax.experimental import pallas as pl
from jax.experimental.pallas import tpu as pltpu
from jax.sharding import PartitionSpec as P

HEAD_DIM = 64
TILE = 128
TOP = 4
BF = jnp.bfloat16
F32 = jnp.float32
VM = pl.BlockSpec(memory_space=pltpu.VMEM)
SM = pl.BlockSpec(memory_space=pltpu.SMEM)
PARAMS = pltpu.CompilerParams(vmem_limit_bytes=32 * 2**20)

YL, XN, CORES, ZN, YH = 4, 4, 2, 8, 2
DP = YL * XN * CORES
SEQ = ZN * YH


def dot(a, b, ca, cb):
    return lax.dot_general(a, b, (((ca,), (cb,)), ((), ())), preferred_element_type=F32)


def flip_y(x):
    return lax.ppermute(x, "seq", [(s, s ^ 1) for s in range(SEQ)])


def shift_z(x, k):
    return lax.ppermute(x, "seq", [(s, (s + YH * k) % SEQ) for s in range(SEQ)])


def swap_dp(x, bit):
    return lax.ppermute(x, "dp", [(d, d ^ bit) for d in range(DP)])


def spread(x, axis, n):
    copies = jnp.broadcast_to(x[None], (n, *x.shape))
    return lax.all_to_all(copies, axis, 0, 0, tiled=True)


def mirror(dp):
    return sum(((dp >> k) & 1) << (4 - k) for k in range(5))


def tiles_of(blocks):
    own, flip, r1, l1, r2, r3, l2, l3, r4, l4, far = blocks
    half = TILE // 2
    yield from (own[...], flip[...], r1[...], l1[...])
    for pair in (r2, r3, l2, l3):
        yield pair[...]
    yield r4[:TILE]
    yield l4[half:]
    yield jnp.concatenate([r4[TILE:], l4[:half]], axis=0)
    yield far[...]


def tile_places(z, y_hi):
    steps = [(0, 0), (0, 1), (-1, 0), (1, 0), (-1, 1), (-2, 0), (-2, 1), (-3, 0)]
    steps += [(2, 0), (1, 1), (3, 0), (2, 1), (-3, 1), (3, 1), (4, 0), (4, 1)]
    places = [lax.rem(z + k + ZN, ZN) * YH + lax.rem(y_hi + j, YH) for k, j in steps]
    return jnp.stack(places).astype(jnp.int32)


def gather_scene(own):
    flip, r1, l1 = flip_y(own), shift_z(own, 1), shift_z(own, -1)
    r2 = shift_z(jnp.concatenate([flip, r1], axis=0), 1)
    l2 = shift_z(jnp.concatenate([l1, flip], axis=0), -1)
    r3, l3 = shift_z(r2, 1), shift_z(l2, -1)
    half = TILE // 2
    r4, l4 = shift_z(r3[: TILE + half], 1), shift_z(l3[half:], -1)
    far = shift_z(flip, ZN // 2)
    return own, flip, r1, l1, r2, r3, l2, l3, r4, l4, far


def attend(nblk, here_ref, order_ref, list_ref, count_ref, *refs):
    blocks = refs[:nblk]
    w_ref, cot_ref, out_ref, keep_ref, send_ref, kv_rows, kv_cols, q_cols, acc = refs[nblk:]
    scale = HEAD_DIM ** (-0.5)
    tiles = kv_rows.shape[0]
    w = w_ref[...]
    w = jnp.concatenate([w[HEAD_DIM:], w[:HEAD_DIM]], axis=0)
    slot = 0
    for blk in tiles_of(blocks):
        qkv = dot(blk, w, 1, 1).astype(BF)
        for r in range(blk.shape[0] // TILE):
            tile = order_ref[slot]
            slot += 1
            piece = qkv[r * TILE : (r + 1) * TILE]
            kv = piece[:, :TILE]
            kv_rows[tile] = kv
            kv_cols[tile] = kv.T
            q_cols[tile] = piece[:, TILE:].T
    acc[...] = jnp.zeros_like(acc)
    zero = jnp.zeros((HEAD_DIM, TILE), BF)

    def step(a, _):
        left = jnp.concatenate([q_cols[a], zero], axis=0)
        right = jnp.concatenate([zero, cot_ref[a, :HEAD_DIM, :]], axis=0)
        both = jnp.concatenate([left, right], axis=1)
        keys = [list_ref[a, t] for t in range(TOP)]
        count = count_ref[a]
        rows = jnp.concatenate([kv_rows[j] for j in keys], axis=0)
        prod = dot(rows, both, 1, 0)
        raw = prod[:, :TILE]
        dprobs = prod[:, TILE:]
        parts = [raw[t * TILE : (t + 1) * TILE] for t in range(TOP)]
        raw = jnp.concatenate(
            parts[:1] + [jnp.where(t < count, parts[t], -1e30) for t in range(1, TOP)], axis=0
        )
        top = jnp.max(raw, axis=0, keepdims=True)
        expo = jnp.exp((raw - top) * scale)
        probs = expo * (1.0 / jnp.sum(expo, axis=0, keepdims=True))
        delta = jnp.sum(probs * dprobs, axis=0, keepdims=True)
        dscores = (probs * ((dprobs - delta) * scale)).astype(BF)
        pair = jnp.concatenate([dscores, probs.astype(BF)], axis=1)
        cols = jnp.concatenate([kv_cols[j] for j in keys], axis=1)
        out = dot(cols, pair, 1, 0)
        out_ref[a, :HEAD_DIM, :] = out[:HEAD_DIM, :TILE].astype(BF)
        out_ref[a, 3 * HEAD_DIM :, :] = out[HEAD_DIM:, TILE:].astype(BF)
        both_t = jnp.concatenate([left.T, right.T], axis=0)
        back = dot(pair, both_t, 1, 0)
        for t in range(TOP):
            acc[keys[t]] += back[t * TILE : (t + 1) * TILE]
        return 0

    lax.fori_loop(0, tiles, step, 0, unroll=2)
    for a in range(tiles):
        out_ref[a, HEAD_DIM : 3 * HEAD_DIM, :] = acc[a].astype(BF).T

    total, slot = None, 0
    for blk in tiles_of(blocks):
        n = blk.shape[0] // TILE
        left = [out_ref[order_ref[slot + r], : 3 * HEAD_DIM, :] for r in range(n)]
        slot += n
        part = dot(jnp.concatenate(left, axis=1), blk, 1, 0)
        total = part if total is None else total + part
    rows = keep_ref.shape[1]
    here = here_ref[0]
    first = here < DP // 2
    for i in range(0, DP, CORES):
        even, odd = total[i * rows : (i + 1) * rows], total[(i + 1) * rows : (i + 2) * rows]
        at = (mirror(i) ^ here) % (DP // 2)
        keep_ref[at] = jnp.where(first, even, odd)
        send_ref[at] = jnp.where(first, odd, even).astype(BF)


def attention(here, order, tile_list, counts, blocks, w_head, cot_t):
    tiles = tile_list.shape[0]
    rows, depth = w_head.shape[0] // DP, w_head.shape[1]
    outs = (
        ((tiles, 4 * HEAD_DIM, TILE), BF),
        ((DP // CORES, rows, depth), F32),
        ((DP // CORES, rows, depth), BF),
    )
    return pl.pallas_call(
        functools.partial(attend, len(blocks)),
        out_shape=tuple(jax.ShapeDtypeStruct(*o) for o in outs),
        out_specs=(VM,) * 3,
        in_specs=[SM, SM, SM, SM] + [VM] * (len(blocks) + 2),
        scratch_shapes=[
            pltpu.VMEM((tiles, TILE, 2 * HEAD_DIM), BF),
            pltpu.VMEM((tiles, 2 * HEAD_DIM, TILE), BF),
            pltpu.VMEM((tiles, HEAD_DIM, TILE), BF),
            pltpu.VMEM((tiles, TILE, 2 * HEAD_DIM), F32),
        ],
        compiler_params=PARAMS,
        name="attend",
    )(here, order, tile_list, counts, *blocks, w_head, cot_t)


def input_sum(both_ref, w_ref, att_ref, out_ref, sorted_ref):
    heads = both_ref.shape[0]
    att_ref[...] = jnp.concatenate(
        [both_ref[h, 3 * HEAD_DIM :, :] for h in range(heads)], axis=0
    ).T
    rows = 3 * HEAD_DIM // DP
    for h in range(heads):
        part = both_ref[h, : 3 * HEAD_DIM, :].astype(F32)
        for d in range(DP):
            at = (d * heads + h) * rows
            sorted_ref[at : at + rows, :] = part[d * rows : (d + 1) * rows]
    left = sorted_ref[...].astype(BF).T
    out_ref[...] = dot(left, w_ref[...], 1, 0).astype(BF)


def input_grad(both, w_all):
    heads = both.shape[0]
    return pl.pallas_call(
        input_sum,
        out_shape=(
            jax.ShapeDtypeStruct((TILE, heads * HEAD_DIM), BF),
            jax.ShapeDtypeStruct((TILE, w_all.shape[1]), BF),
        ),
        in_specs=[VM, VM],
        out_specs=(VM, VM),
        scratch_shapes=[pltpu.VMEM((w_all.shape[0], TILE), F32)],
        compiler_params=PARAMS,
        name="input_sum",
    )(both, w_all)


def shards(tokens, qkv_weight, key_tiles, key_counts, cotangent):
    heads = SEQ
    depth = tokens.shape[2]
    tiles = key_tiles.shape[1]
    dp, seq = lax.axis_index("dp"), lax.axis_index("seq")
    z, y_hi = seq // YH, seq % YH
    grad_scale = (DP * tiles * TILE) ** (-0.5)

    blocks = gather_scene(tokens[0])

    own_rows = qkv_weight[0]
    rows = own_rows.shape[0]
    lanes = rows * depth // TILE
    cot_t = cotangent[0].T.reshape(heads, HEAD_DIM, TILE)
    copies = jnp.broadcast_to(own_rows.reshape(lanes, TILE)[None], (heads, lanes, TILE))
    mixed = jnp.concatenate([cot_t, copies], axis=1)
    mixed = lax.all_to_all(mixed, "seq", 0, 0, tiled=True)
    w_seq = mixed[:, HEAD_DIM:].reshape(heads * rows, depth)
    w_seq, _ = lax.optimization_barrier((w_seq, (blocks[4], blocks[6])))
    w_all = lax.all_gather(w_seq, "dp", axis=0, tiled=True)

    own_rows, _ = lax.optimization_barrier((own_rows, mixed))
    w_head = spread(own_rows, "dp", DP).reshape(DP * rows, depth)

    here = mirror(dp)[None].astype(jnp.int32)
    order = tile_places(z, y_hi)
    both, keep, send = attention(here, order, key_tiles[0], key_counts[0], blocks, w_head, mixed)
    both = lax.all_to_all(both, "seq", 0, 0, tiled=True)

    came = swap_dp(send, 1)
    for bit in (2, 4, 8, 16):
        if bit == 16:
            w_all, came = lax.optimization_barrier((w_all, came))
        half = keep.shape[0] // 2
        send = (keep[half:] + came[half:].astype(F32)).astype(BF)
        keep = keep[:half] + came[:half].astype(F32)
        came = swap_dp(send, bit)
    grad_weight = (keep + came.astype(F32)) * grad_scale

    attended, grad_input = input_grad(both, w_all)
    return (attended[None], grad_input[None], grad_weight)


def solution(mesh):
    in_specs = (
        P("dp", "seq", None),
        P("seq", "dp", None),
        P("dp", None, None),
        P("dp", None),
        P("dp", "seq", None),
    )
    out_specs = (P("dp", "seq", None), P("dp", "seq", None), P("seq", "dp", None))
    return jax.shard_map(shards, mesh=mesh, in_specs=in_specs, out_specs=out_specs, check_vma=False)
```
